32 devices in a mesh: wide: 4 (over y, core), narrow: 8 (over z, x).
Axes of the slice: x: 2, y: 2, z: 4, core: 2. Of those that a mesh axis runs over, the one named last changes fastest.
Arguments:
- site_basis: bfloat16 [512, 512], P(('wide', 'narrow')), may hold values from -0.25 to 0.25
- left_ops: bfloat16 [96, 512, 512], P(('wide', 'narrow')), may hold values from -0.25 to 0.25
- right_ops: bfloat16 [96, 512, 512], P(('wide', 'narrow')), may hold values from -0.25 to 0.25
- integrals: bfloat16 [96, 96], replicated, may hold values from -0.625 to 0.625
- wavefunction: bfloat16 [512, 512], P(('wide', 'narrow')), may hold values from -6 to 6
- pair_order: int32 [96], replicated, may hold values from 0 to 95, each once
- sector_sizes: int32 [8], replicated, may hold values from 1 to 128, 512 in all
Outputs:
- propagated: float32 [512, 512], P(('wide', 'narrow'))
The draws below stay inside these ranges and needn't reach their ends.
Inputs may be any that keep to these rules, and one draw needn't show every extreme that they name: `pair_order`: each orbital pair stands in exactly one of the 96 slots. `sector_sizes`: the sizes sum to 512.
All inputs are finite; a program needn't handle non-finite values.
Results may differ from the reference program's by a relative error of at most 0.008.
Values may be sent and summed in bfloat16 or wider, within the bound.
No kernel may reach another device: no remote copies, remote signals or barrier semaphores. Data moves between devices by JAX's collectives and lax.ppermute only.
A program may use at most 64 MiB of HBM per device.

```python
import math
import jax
import jax.numpy as jnp
import numpy as np
from jax import lax

M = 512
ORDER = 3
BLOCKS = 8
PAIRS = 96


def steps_of(rng, shape, split, low, largest):
    gain = 1.0
    for dim, shards_of in split:
        steps = jax.random.uniform(jax.random.fold_in(jax.random.fold_in(rng, 6), dim), (shards_of,), jnp.float32, low / len(split), largest / len(split))
        gain = gain * jnp.repeat(jnp.exp(steps), shape[dim] // shards_of).reshape((-1,) + (1,) * (len(shape) - 1 - dim))
    return gain


def length_profile(count, total, reach, slope):
    weights = [(1 << 20) // math.isqrt(grade ** slope) + 1 for grade in range(2, count + 1)]
    surplus, holding = total - reach - (count - 1), [1] * (count - 1)
    while surplus > 0:
        movable = [i for i in range(count - 1) if holding[i] < reach]
        mass, remaining = sum([weights[i] for i in movable]), surplus
        for i in movable:
            addition = min(reach - holding[i], max(1, remaining * weights[i] // mass), surplus)
            holding[i] = holding[i] + addition
            surplus = surplus - addition
    return np.array([reach] + holding)


def ragged(own_key, number_of, total, reach, skew):
    if number_of == 2:
        one = jax.random.randint(own_key, (), max(1, total - reach), min(reach, total - 1) + 1)
        return jnp.stack([one, total - one])
    tallies = jnp.asarray(length_profile(number_of, total, reach, skew), jnp.int32)
    twos = (number_of - 1) // 2
    source_of, taker = tallies[1:1 + 2 * twos:2], tallies[2:2 + 2 * twos:2]
    slack = jnp.minimum(source_of - 1, reach - taker)
    moved = jax.random.randint(jax.random.fold_in(own_key, 1), (twos,), 0, 1 << 20) % (slack + 1)
    tallies = tallies.at[1:1 + 2 * twos:2].set(source_of - moved).at[2:2 + 2 * twos:2].set(taker + moved)
    return tallies[jax.random.permutation(jax.random.fold_in(own_key, 2), number_of)]


def bell_draw(own_key, dims, spread, bound, split=(), kind=jnp.bfloat16):
    result = jax.random.normal(own_key, dims, jnp.float32) * spread
    if len(split) > 0:
        result = steps_of(own_key, dims, split, -0.22, 0.18) * result
    return jnp.clip(result, min=-bound, max=bound).astype(kind)


def setup_inputs(seed: int = 0) -> dict:
    arg_keys = jax.random.split(jax.random.key(seed), 8)
    site_basis = bell_draw(arg_keys[0], (M, M), M ** -0.5, 0.25, ((0, 32),))
    left_ops = bell_draw(arg_keys[1], (PAIRS, M, M), M ** -0.5, 0.25, ((0, 32),))
    right_ops = bell_draw(arg_keys[2], (PAIRS, M, M), M ** -0.5, 0.25, ((0, 32),))
    integrals = bell_draw(arg_keys[3], (PAIRS, PAIRS), PAIRS ** -0.5, 0.625)
    wavefunction = bell_draw(arg_keys[4], (M, M), 1.0, 6.0, ((0, 32),))
    pair_order = jax.random.permutation(arg_keys[5], PAIRS).astype(jnp.int32)
    sector_sizes = ragged(arg_keys[6], BLOCKS, M, M // 4, 2).astype(jnp.int32)
    return dict(site_basis=site_basis, left_ops=left_ops, right_ops=right_ops, integrals=integrals, wavefunction=wavefunction, pair_order=pair_order, sector_sizes=sector_sizes)


def sector_mask(sector_sizes, row_ids, col_ids):
    block_ends = jnp.cumsum(sector_sizes).astype(jnp.int32)
    row_block = lax.optimization_barrier(jnp.sum((row_ids[:, None] >= block_ends[None, :]).astype(jnp.int32), axis=1))
    col_block = lax.optimization_barrier(jnp.sum((col_ids[:, None] >= block_ends[None, :]).astype(jnp.int32), axis=1))
    return (jnp.abs(row_block[:, None] - col_block[None, :]) <= 2).astype(jnp.float32)

def product(left, right):
    return jnp.dot(left.astype(jnp.float32), right.astype(jnp.float32), precision=lax.Precision.HIGHEST)

def reference(site_basis, left_ops, right_ops, integrals, wavefunction, pair_order, sector_sizes):

    def build(left_one):
        rotated = product(left_one, site_basis).astype(jnp.bfloat16)
        return product(site_basis.T, rotated).astype(jnp.bfloat16)
    built_ops = lax.map(build, left_ops)
    mixing = jnp.take(jnp.take(integrals, pair_order, axis=0), pair_order, axis=1)
    comp_ops = product(mixing, right_ops.reshape(PAIRS, M * M))
    comp_ops = comp_ops.astype(jnp.bfloat16).reshape(PAIRS, M, M)
    states = jnp.arange(M, dtype=jnp.int32)
    masking = sector_mask(sector_sizes, states, states)
    state = (wavefunction.astype(jnp.float32) * masking).astype(jnp.bfloat16)
    summed = state.astype(jnp.float32)
    step_size = 2.0 / math.sqrt(PAIRS)
    for order_index in range(1, ORDER + 1):

        def accumulate(carry, pair_ops, current=state):
            left_one, right_one = pair_ops
            applied = product(left_one, current).astype(jnp.bfloat16)
            return (carry + product(applied, right_one.T), None)
        full_term, _ = lax.scan(accumulate, jnp.zeros((M, M), jnp.float32), (built_ops, comp_ops))
        state = (-(step_size / order_index) * masking * full_term).astype(jnp.bfloat16)
        summed = summed + state.astype(jnp.float32)
    return summed
```

```python
import functools
import math

import jax
import jax.numpy as jnp
from jax import lax
from jax.experimental import pallas as pl
from jax.experimental.pallas import tpu as pltpu
from jax.sharding import Mesh, PartitionSpec as P

ORDER = 3
OUTER, CORE, NARROW = "outer", "core", "narrow"
ALL = (OUTER, CORE, NARROW)
CHIPS = (OUTER, NARROW)
VMEM_LIMIT = 48 * 1024 * 1024
F32, BF16 = jnp.float32, jnp.bfloat16


def whole_block(shape):
    return pl.BlockSpec(shape, lambda *_: (0,) * len(shape))


def kernel_params():
    return pltpu.CompilerParams(vmem_limit_bytes=VMEM_LIMIT)


def block_ids(sector_sizes, count):
    ends = jnp.cumsum(sector_sizes)
    ids = jnp.arange(count, dtype=jnp.int32)
    return jnp.sum((ids[:, None] >= ends[None, :]).astype(jnp.int32), axis=1)


def swap_cores(value):
    return lax.ppermute(value, CORE, [(0, 1), (1, 0)])


def gather_over(value, axis, size):
    value = value[None]
    if size & (size - 1):
        return lax.all_gather(value, axis, axis=0, tiled=True)
    position = lax.axis_index(axis)
    if size == 1:
        return value
    steps = [1 << bit for bit in range(size.bit_length() - 1)]
    done = []
    for step in steps[1:] + steps[:1]:
        got = lax.ppermute(value, axis, [(i, i ^ step) for i in range(size)])
        high = (position // step) % 2 == 1
        low_part = jnp.where(high, got, value)
        high_part = jnp.where(high, value, got)
        value = jnp.stack([low_part, high_part])
        done = [step] + done
    bits = len(done)
    tail = value.shape[bits + 1 :]
    value = value.reshape((2,) * bits + tail)
    order = sorted(range(bits), key=lambda dim: -done[dim])
    value = value.transpose(tuple(order) + tuple(range(bits, bits + len(tail))))
    return value.reshape((size,) + tail)


def build_kernel(basis_ref, left_ref, built_ref):
    basis = basis_ref[...]
    rotated = jnp.dot(left_ref[0], basis, preferred_element_type=F32).astype(BF16)
    built = lax.dot_general(basis, rotated, (((0,), (0,)), ((), ())), preferred_element_type=F32)
    built_ref[0] = built.astype(BF16)


def build(basis, left_ops):
    pairs, states, _ = left_ops.shape
    flops = 4 * pairs * states**3
    return pl.pallas_call(
        build_kernel,
        grid=(pairs,),
        in_specs=[
            whole_block((states, states)),
            pl.BlockSpec((1, states, states), lambda s: (s, 0, 0)),
        ],
        out_specs=pl.BlockSpec((1, states, states), lambda s: (s, 0, 0)),
        out_shape=jax.ShapeDtypeStruct(left_ops.shape, BF16),
        compiler_params=kernel_params(),
        cost_estimate=pl.CostEstimate(flops=flops, bytes_accessed=4 * left_ops.size, transcendentals=0),
        name="build",
    )(basis, left_ops)


def spread_kernel(rows, row_pair_ref, col_pair_ref, integrals_ref, spread_ref):
    height, width = spread_ref.shape
    total = integrals_ref.shape[0]
    pick_row = (row_pair_ref[...] == lax.broadcasted_iota(jnp.int32, (height, total), 1)).astype(F32)
    pick_col = (col_pair_ref[...] == lax.broadcasted_iota(jnp.int32, (total, width), 0)).astype(F32)
    picked = jnp.dot(pick_row.astype(BF16), integrals_ref[...], preferred_element_type=F32)
    mixing = jnp.dot(picked.astype(BF16), pick_col.astype(BF16), preferred_element_type=F32)
    row_id = lax.broadcasted_iota(jnp.int32, (height, width), 0) + pl.program_id(0) * height
    col_id = lax.broadcasted_iota(jnp.int32, (height, width), 1)
    same = lax.rem(row_id, rows) == lax.rem(col_id, rows)
    spread_ref[...] = jnp.where(same, mixing, 0.0).astype(BF16)


def spread_mixing(integrals, pair_order, rows, parts):
    total = integrals.shape[0]
    size = total * rows
    height = size // parts
    repeated = jnp.repeat(pair_order, rows)
    return pl.pallas_call(
        functools.partial(spread_kernel, rows),
        grid=(parts,),
        in_specs=[
            pl.BlockSpec((height, 1), lambda w: (w, 0)),
            whole_block((1, size)),
            whole_block((total, total)),
        ],
        out_specs=pl.BlockSpec((height, size), lambda w: (w, 0)),
        out_shape=jax.ShapeDtypeStruct((size, size), BF16),
        compiler_params=kernel_params(),
        cost_estimate=pl.CostEstimate(flops=2 * size * size * total, bytes_accessed=2 * size * size, transcendentals=0),
        name="spread_mixing",
    )(repeated[:, None], repeated[None, :], integrals)


def mix_kernel(spread_ref, right_ref, out_ref):
    mixed = jnp.dot(spread_ref[...], right_ref[...], preferred_element_type=F32).astype(BF16)
    narrow, block, half = out_ref.shape[2], out_ref.shape[4], out_ref.shape[5]
    for h in range(2):
        out_ref[0, h, :, 0] = mixed[:, h * half : (h + 1) * half].reshape(narrow, block, half)


def mix(spread, right_rows, wide, narrow, block):
    size, states = right_rows.shape
    height = size // wide
    half = states // 2
    if block % 16:
        mixed = jnp.dot(spread, right_rows, preferred_element_type=F32).astype(BF16)
        mixed = mixed.reshape(wide // 2, 2, narrow, block, 2, half)
        return mixed.transpose(0, 4, 2, 1, 3, 5)
    return pl.pallas_call(
        mix_kernel,
        grid=(wide,),
        in_specs=[
            pl.BlockSpec((height, size), lambda w: (w, 0)),
            whole_block((size, states)),
        ],
        out_specs=pl.BlockSpec((1, 2, narrow, 1, block, half), lambda w: (w // 2, 0, 0, w % 2, 0, 0)),
        out_shape=jax.ShapeDtypeStruct((wide // 2, 2, narrow, 2, block, half), BF16),
        compiler_params=kernel_params(),
        cost_estimate=pl.CostEstimate(flops=2 * size * size * states, bytes_accessed=2 * size * size, transcendentals=0),
        name="mix",
    )(spread, right_rows)


def apply_kernel(core_ref, state_ref, own_ref, other_ref, comp_ref, keep_ref, send_ref, applied_ref):
    outer, narrow, _, rows, half = state_ref.shape
    pairs, states, _ = own_ref.shape
    chips = outer * narrow
    core = core_ref[0]
    state = jnp.concatenate(
        [state_ref[y, :, c].reshape(narrow * rows, half) for y in range(outer) for c in range(2)]
    )
    for side, ref in enumerate((own_ref, other_ref)):
        for q in range(pairs):
            one = jnp.dot(ref[q], state, preferred_element_type=F32).astype(BF16)
            column = (side * pairs + q) * half
            applied_ref[:, column : column + half] = one
    applied = applied_ref[...]
    for out_ref, place in ((send_ref, 1 - core), (keep_ref, core)):
        columns = []
        for side in (core, 1 - core):
            for q in range(pairs):
                part = comp_ref[pl.ds(place * chips, chips), side * pairs + q]
                columns.append(part.reshape(chips * rows, half))
        joined = jnp.concatenate(columns, axis=1)
        term = lax.dot_general(applied, joined, (((1,), (1,)), ((), ())), preferred_element_type=F32)
        term = term.astype(out_ref.dtype).reshape(outer, 2, narrow, rows, half)
        for c in range(2):
            out_ref[:, :, c] = term[:, c]


def apply_pairs(core, state, own, other, comp):
    outer, narrow, _, rows, half = state.shape
    pairs, states, _ = own.shape
    if rows % 16:
        full = state.transpose(0, 2, 1, 3, 4).reshape(states, half)
        built = jnp.concatenate([own, other])
        applied = jnp.einsum("sil,lk->sik", built, full, preferred_element_type=F32).astype(BF16)
        joined = comp.transpose(1, 0, 2, 3).reshape(2, pairs, states, half)
        joined = jnp.concatenate([joined[core[0]], joined[1 - core[0]]])
        term = jnp.einsum("sik,sjk->ij", applied, joined, preferred_element_type=F32)
        term = term.reshape(outer, 2, narrow, rows, 2, half).transpose(4, 0, 2, 1, 3, 5)
        return term[core[0]], term[1 - core[0]].astype(BF16)
    return pl.pallas_call(
        apply_kernel,
        in_specs=[pl.BlockSpec(memory_space=pltpu.SMEM)] + [pl.BlockSpec(memory_space=pltpu.VMEM)] * 4,
        out_specs=[pl.BlockSpec(memory_space=pltpu.VMEM)] * 2,
        out_shape=[
            jax.ShapeDtypeStruct(state.shape, F32),
            jax.ShapeDtypeStruct(state.shape, BF16),
        ],
        scratch_shapes=[pltpu.VMEM((states, 2 * pairs * half), BF16)],
        compiler_params=kernel_params(),
        cost_estimate=pl.CostEstimate(
            flops=8 * pairs * states**2 * half, bytes_accessed=8 * pairs * states**2, transcendentals=0
        ),
        name="apply_pairs",
    )(core, state, own, other, comp)


def local(site_basis, left_ops, right_ops, integrals, wavefunction, pair_order, sector_sizes):
    outer, narrow = lax.axis_size(OUTER), lax.axis_size(NARROW)
    wide = 2 * outer
    devices = wide * narrow
    rows, states = wavefunction.shape
    half = states // 2
    pairs = left_ops.shape[0]
    pair_total = integrals.shape[0]
    chips = outer * narrow
    own_outer, own_core, own_narrow = (lax.axis_index(name) for name in ALL)
    is_high = own_core == 1

    def own_half(value):
        return jnp.where(is_high, value[..., half:], value[..., :half])

    def other_half(value):
        return jnp.where(is_high, value[..., :half], value[..., half:])

    def by_core(own, other):
        return jnp.stack([jnp.where(is_high, other, own), jnp.where(is_high, own, other)])

    parts = right_ops.reshape(pairs, devices, rows, states).transpose(1, 0, 2, 3)
    parts = parts.reshape(devices, pairs * rows, states)
    right_rows = lax.all_to_all(parts, ALL, split_axis=0, concat_axis=0, tiled=True)
    right_rows = right_rows.reshape(pair_total * rows, states)
    spread = spread_mixing(integrals, pair_order, rows, wide)

    blocks = block_ids(sector_sizes, states).astype(F32)
    by_device = blocks.reshape(outer, 2, narrow, rows)
    chip_rows = lax.dynamic_slice(by_device, (own_outer, 0, own_narrow, 0), (1, 2, 1, rows)).reshape(2, rows)
    own_columns = own_half(blocks)
    local_mask = (jnp.abs(chip_rows[:, :, None] - own_columns[None, None, :]) <= 2.0).astype(F32)

    piece = by_core(own_half(wavefunction), swap_cores(other_half(wavefunction)))
    piece = (piece.astype(F32) * local_mask).astype(BF16)
    summed = piece.astype(F32)

    together = jnp.concatenate([site_basis.reshape(rows * 2, half), piece.reshape(2 * rows, half)])
    gathered = gather_over(gather_over(together, NARROW, narrow), OUTER, outer)
    basis_rows = gathered[:, :, : 2 * rows].reshape(outer, narrow, rows, states)
    state = gathered[:, :, 2 * rows :].reshape(outer, narrow, 2, rows, half)
    basis = by_core(basis_rows, swap_cores(basis_rows))
    basis = basis.transpose(1, 0, 2, 3, 4).reshape(states, states)
    own_built = build(basis, left_ops)
    other_built = swap_cores(own_built)

    mixed = mix(spread, right_rows, wide, narrow, pairs * rows)
    mixed = mixed.reshape(devices, 2 * pairs * rows, half)
    comp = lax.all_to_all(mixed, ALL, split_axis=0, concat_axis=0, tiled=True)
    comp = comp.reshape(devices, 2 * pairs, rows, half)

    step_size = 2.0 / math.sqrt(pair_total)
    core = own_core.reshape(1)
    for order_index in range(1, ORDER + 1):
        keep, send = apply_pairs(core, state, own_built, other_built, comp)
        partial = (keep + swap_cores(send).astype(F32)).astype(BF16)
        partial = partial.reshape(chips, 2 * rows, half)
        arrived = lax.all_to_all(partial, CHIPS, split_axis=0, concat_axis=0, tiled=True)
        term = jnp.sum(arrived.astype(F32), axis=0).reshape(2, rows, half)
        piece = (-(step_size / order_index) * local_mask * term).astype(BF16)
        summed = summed + piece.astype(F32)
        if order_index < ORDER:
            copies = jnp.broadcast_to(piece.reshape(1, 2 * rows, half), (chips, 2 * rows, half))
            state = lax.all_to_all(copies, CHIPS, split_axis=0, concat_axis=0, tiled=True)
            state = state.reshape(outer, narrow, 2, rows, half)

    mine = jnp.where(is_high, summed[1], summed[0])
    theirs = jnp.where(is_high, summed[0], summed[1])
    left, right = by_core(mine, swap_cores(theirs))
    return jnp.concatenate([left, right], axis=1)


def solution(mesh):
    wide, narrow = mesh.shape["wide"], mesh.shape["narrow"]
    finer = Mesh(mesh.devices.reshape(wide // 2, 2, narrow), ALL)
    placed = (
        P(ALL, None),
        P(ALL, None, None),
        P(ALL, None, None),
        P(),
        P(ALL, None),
        P(),
        P(),
    )
    return jax.shard_map(local, mesh=finer, in_specs=placed, out_specs=P(ALL, None), check_vma=False)
```

```python
import functools
import math

import jax
import jax.numpy as jnp
from jax import lax
from jax.experimental import pallas as pl
from jax.experimental.pallas import tpu as pltpu
from jax.sharding import Mesh, PartitionSpec as P

ORDER = 3
OUTER, CORE, FAR, NEAR = "outer", "core", "far", "near"
ALL = (OUTER, CORE, FAR, NEAR)
CHIPS = (OUTER, FAR, NEAR)
MIB = 1024 * 1024
LANES = 128
IN_HBM, IN_VMEM = pl.BlockSpec(memory_space=pltpu.HBM), pl.BlockSpec(memory_space=pltpu.VMEM)
F32, BF16 = jnp.float32, jnp.bfloat16


def whole_block(shape):
    return pl.BlockSpec(shape, lambda *_: (0,) * len(shape))


def kernel_params(mib):
    return pltpu.CompilerParams(vmem_limit_bytes=mib * MIB)


def block_ids(sector_sizes, count):
    ends = jnp.cumsum(sector_sizes)
    ids = jnp.arange(count, dtype=jnp.int32)
    return jnp.sum((ids[:, None] >= ends[None, :]).astype(jnp.int32), axis=1)


def swap_cores(value):
    return lax.ppermute(value, CORE, [(0, 1), (1, 0)])


def gather_over(value, axes, size):
    if size & (size - 1):
        return lax.all_gather(value, axes)
    position = lax.axis_index(axes)
    slots = [value]
    for k in range(1, size):
        slots.append(lax.ppermute(value, axes, [(i, i ^ k) for i in range(size)]))
    gathered = jnp.stack(slots)
    for bit in range(size.bit_length() - 1):
        pairs = gathered.reshape((-1, 2, 1 << bit) + value.shape)
        pairs = jnp.where((position >> bit) % 2 == 1, pairs[:, ::-1], pairs)
        gathered = pairs.reshape(gathered.shape)
    return gathered


def deal_kernel(right_ref, out_ref, held, in_sems, out_sems):
    pairs = held.shape[0]
    loads = [pltpu.make_async_copy(right_ref.at[s], held.at[s], in_sems.at[s]) for s in range(pairs)]
    stores = [
        pltpu.make_async_copy(held.at[s], out_ref.at[:, s], out_sems.at[s]) for s in range(pairs)
    ]
    for load in loads:
        load.start()
    for load, store in zip(loads, stores):
        load.wait()
        store.start()
    for store in stores:
        store.wait()


def deal_rows(right_ops, devices):
    pairs, states, _ = right_ops.shape
    rows = states // devices
    split = right_ops.reshape(pairs, devices, rows, states)
    if rows % 16:
        return split.transpose(1, 0, 2, 3)
    return pl.pallas_call(
        deal_kernel,
        in_specs=[IN_HBM],
        out_specs=IN_HBM,
        out_shape=jax.ShapeDtypeStruct((devices, pairs, rows, states), BF16),
        scratch_shapes=[
            pltpu.VMEM(split.shape, BF16),
            pltpu.SemaphoreType.DMA((pairs,)),
            pltpu.SemaphoreType.DMA((pairs,)),
        ],
        compiler_params=kernel_params(2),
        name="deal_rows",
    )(split)


def build_kernel(basis_ref, left_ref, built_ref):
    basis = basis_ref[...]
    rotated = jnp.dot(left_ref[0], basis, preferred_element_type=F32).astype(BF16)
    built = lax.dot_general(basis, rotated, (((0,), (0,)), ((), ())), preferred_element_type=F32)
    built_ref[0] = built.astype(BF16)


def build(basis, left_ops):
    pairs, states, _ = left_ops.shape
    return pl.pallas_call(
        build_kernel,
        grid=(pairs,),
        in_specs=[
            whole_block((states, states)),
            pl.BlockSpec((1, states, states), lambda s: (s, 0, 0)),
        ],
        out_specs=pl.BlockSpec((1, states, states), lambda s: (s, 0, 0)),
        out_shape=jax.ShapeDtypeStruct(left_ops.shape, BF16),
        compiler_params=kernel_params(12),
        cost_estimate=pl.CostEstimate(flops=0, bytes_accessed=0, transcendentals=0),
        name="build",
    )(basis, left_ops)


def mix_kernel(mixing_ref, right_ref, out_ref, taken, given, mixed, sems):
    total = mixing_ref.shape[0]
    wide, narrow, block, half = mixed.shape[1:]
    rows = right_ref.shape[0] // total
    lanes = half // LANES
    mixing = mixing_ref[...]
    stores = [
        pltpu.make_async_copy(mixed.at[h, w], out_ref.at[w // 2, h, :, w % 2], sems.at[h, w])
        for h in range(2)
        for w in range(wide)
    ]
    for h in range(2):
        places = range(h * lanes, (h + 1) * lanes)
        for place in places:
            taken[place] = right_ref[:, place * LANES : (place + 1) * LANES].astype(F32)
        for row in range(rows):
            every = pl.ds(row, total, stride=rows)
            one = jnp.concatenate([taken[place, every] for place in places], axis=1).astype(BF16)
            one = jnp.dot(mixing, one, preferred_element_type=F32)
            for lane, place in enumerate(places):
                given[place, every] = one[:, lane * LANES : (lane + 1) * LANES]
        for lane, place in enumerate(places):
            done = given[place].astype(BF16).reshape(wide, narrow, block, LANES)
            mixed[h, :, :, :, lane * LANES : (lane + 1) * LANES] = done
        for w in range(wide):
            stores[h * wide + w].start()
    for store in stores:
        store.wait()


def mix(mixing, right_rows, wide, narrow, block):
    size, states = right_rows.shape
    total = mixing.shape[0]
    half = states // 2
    if block % 16:
        mixed = jnp.einsum(
            "st,tx->sx", mixing, right_rows.reshape(total, -1), preferred_element_type=F32
        )
        mixed = mixed.astype(BF16).reshape(wide // 2, 2, narrow, block, 2, half)
        return mixed.transpose(0, 4, 2, 1, 3, 5)
    return pl.pallas_call(
        mix_kernel,
        in_specs=[IN_VMEM, IN_VMEM],
        out_specs=IN_HBM,
        out_shape=jax.ShapeDtypeStruct((wide // 2, 2, narrow, 2, block, half), BF16),
        scratch_shapes=[
            pltpu.VMEM((states // LANES, size, LANES), F32),
            pltpu.VMEM((states // LANES, size, LANES), F32),
            pltpu.VMEM((2, wide, narrow, block, half), BF16),
            pltpu.SemaphoreType.DMA((2, wide)),
        ],
        compiler_params=kernel_params(16),
        cost_estimate=pl.CostEstimate(flops=2 * size * total * states, bytes_accessed=4 * size * states, transcendentals=0),
        name="mix",
    )(mixing, right_rows)


def fetch_kernel(core_ref, state_ref, own_hbm, other_ref, comp_ref, keep_ref, send_ref, applied_ref, own_ref, sem):
    load = pltpu.make_async_copy(own_hbm, own_ref, sem)
    load.start()
    apply_kernel(core_ref, state_ref, own_ref, other_ref, comp_ref, keep_ref, send_ref, applied_ref, load)


def apply_kernel(core_ref, state_ref, own_ref, other_ref, comp_ref, keep_ref, send_ref, applied_ref, load=None):
    outer, narrow, _, rows, half = state_ref.shape
    pairs = own_ref.shape[0]
    chips = outer * narrow
    core = core_ref[0]
    state = jnp.concatenate(
        [state_ref[y, :, c].reshape(narrow * rows, half) for y in range(outer) for c in range(2)]
    )
    for side, ref in ((1, other_ref), (0, own_ref)):
        if side == 0 and load is not None:
            load.wait()
        for q in range(pairs):
            one = jnp.dot(ref[q], state, preferred_element_type=F32).astype(BF16)
            column = (side * pairs + q) * half
            applied_ref[:, column : column + half] = one
    applied = applied_ref[...]
    for out_ref, place in ((send_ref, 1 - core), (keep_ref, core)):
        columns = []
        for side in (core, 1 - core):
            for q in range(pairs):
                part = comp_ref[pl.ds(place * chips, chips), side * pairs + q]
                columns.append(part.reshape(chips * rows, half))
        joined = jnp.concatenate(columns, axis=1)
        term = lax.dot_general(applied, joined, (((1,), (1,)), ((), ())), preferred_element_type=F32)
        term = term.astype(out_ref.dtype).reshape(outer, 2, narrow, rows, half)
        for c in range(2):
            out_ref[:, :, c] = term[:, c]


def apply_pairs(core, state, own, other, comp, fetch):
    outer, narrow, _, rows, half = state.shape
    pairs, states, _ = own.shape
    if rows % 16:
        full = state.transpose(0, 2, 1, 3, 4).reshape(states, half)
        built = jnp.concatenate([own, other])
        applied = jnp.einsum("sil,lk->sik", built, full, preferred_element_type=F32).astype(BF16)
        joined = comp.transpose(1, 0, 2, 3).reshape(2, pairs, states, half)
        joined = jnp.concatenate([joined[core[0]], joined[1 - core[0]]])
        term = jnp.einsum("sik,sjk->ij", applied, joined, preferred_element_type=F32)
        term = term.reshape(outer, 2, narrow, rows, 2, half).transpose(4, 0, 2, 1, 3, 5)
        return term[core[0]], term[1 - core[0]].astype(BF16)
    scratch = [pltpu.VMEM((states, 2 * pairs * half), BF16)]
    if fetch:
        scratch += [pltpu.VMEM(own.shape, BF16), pltpu.SemaphoreType.DMA]
    return pl.pallas_call(
        fetch_kernel if fetch else apply_kernel,
        in_specs=[pl.BlockSpec(memory_space=pltpu.SMEM), IN_VMEM, IN_HBM if fetch else IN_VMEM, IN_VMEM, IN_VMEM],
        out_specs=[IN_VMEM] * 2,
        out_shape=[
            jax.ShapeDtypeStruct(state.shape, F32),
            jax.ShapeDtypeStruct(state.shape, BF16),
        ],
        scratch_shapes=scratch,
        compiler_params=kernel_params(58 if fetch else 12),
        cost_estimate=pl.CostEstimate(
            flops=8 * pairs * states**2 * half, bytes_accessed=8 * pairs * states**2, transcendentals=0
        ),
        name="apply_pairs",
    )(core, state, own, other, comp)


def local(site_basis, left_ops, right_ops, integrals, wavefunction, pair_order, sector_sizes):
    outer, far, near = (lax.axis_size(name) for name in CHIPS)
    narrow = far * near
    wide = 2 * outer
    devices = wide * narrow
    rows, states = wavefunction.shape
    half = states // 2
    pairs = left_ops.shape[0]
    pair_total = integrals.shape[0]
    chips = outer * narrow
    own_outer, own_core, own_narrow = (lax.axis_index(name) for name in (OUTER, CORE, (FAR, NEAR)))
    is_high = own_core == 1

    def own_half(value):
        return jnp.where(is_high, value[..., half:], value[..., :half])

    def other_half(value):
        return jnp.where(is_high, value[..., :half], value[..., half:])

    def by_core(own, other):
        return jnp.stack([jnp.where(is_high, other, own), jnp.where(is_high, own, other)])

    parts = deal_rows(right_ops, devices).reshape(devices, pairs * rows, states)
    parts, wavefunction, site_basis = lax.optimization_barrier((parts, wavefunction, site_basis))
    right_rows = lax.all_to_all(parts, ALL, split_axis=0, concat_axis=0, tiled=True)
    right_rows = right_rows.reshape(pair_total * rows, states)
    mixing = jnp.take(jnp.take(integrals, pair_order, axis=0), pair_order, axis=1)

    blocks = block_ids(sector_sizes, states).astype(F32)
    by_device = blocks.reshape(outer, 2, narrow, rows)
    chip_rows = lax.dynamic_slice(by_device, (own_outer, 0, own_narrow, 0), (1, 2, 1, rows)).reshape(2, rows)
    own_columns = own_half(blocks)
    local_mask = (jnp.abs(chip_rows[:, :, None] - own_columns[None, None, :]) <= 2.0).astype(F32)

    piece = by_core(own_half(wavefunction), swap_cores(other_half(wavefunction)))
    piece = (piece.astype(F32) * local_mask).astype(BF16)
    summed = piece.astype(F32)

    together = jnp.concatenate([site_basis.reshape(rows * 2, half), piece.reshape(2 * rows, half)])
    mixed = mix(mixing, right_rows, wide, narrow, pairs * rows)
    gathered, mixed = lax.optimization_barrier((gather_over(together, FAR, far), mixed))
    gathered = gather_over(gathered, (OUTER, NEAR), outer * near)
    gathered = gathered.reshape(outer, near, far, 4 * rows, half).transpose(0, 2, 1, 3, 4)
    basis_rows = gathered[..., : 2 * rows, :].reshape(outer, narrow, rows, states)
    state = gathered[..., 2 * rows :, :].reshape(outer, narrow, 2, rows, half)
    basis = by_core(basis_rows, swap_cores(basis_rows))
    basis = basis.transpose(1, 0, 2, 3, 4).reshape(states, states)
    own_built = build(basis, left_ops)
    other_built = swap_cores(own_built)

    mixed = mixed.reshape(devices, 2 * pairs * rows, half)
    comp = lax.all_to_all(mixed, ALL, split_axis=0, concat_axis=0, tiled=True)
    comp = comp.reshape(devices, 2 * pairs, rows, half)

    step_size = 2.0 / math.sqrt(pair_total)
    core = own_core.reshape(1)
    for order_index in range(1, ORDER + 1):
        keep, send = apply_pairs(core, state, own_built, other_built, comp, False)
        partial = (keep + swap_cores(send).astype(F32)).astype(BF16)
        partial = partial.reshape(chips, 2 * rows, half)
        arrived = lax.all_to_all(partial, CHIPS, split_axis=0, concat_axis=0, tiled=True)
        term = jnp.sum(arrived.astype(F32), axis=0).reshape(2, rows, half)
        piece = (-(step_size / order_index) * local_mask * term).astype(BF16)
        summed = summed + piece.astype(F32)
        if order_index < ORDER:
            copies = jnp.broadcast_to(piece.reshape(1, 2 * rows, half), (chips, 2 * rows, half))
            state = lax.all_to_all(copies, CHIPS, split_axis=0, concat_axis=0, tiled=True)
            state = state.reshape(outer, narrow, 2, rows, half)

    mine = jnp.where(is_high, summed[1], summed[0])
    theirs = jnp.where(is_high, summed[0], summed[1])
    left, right = by_core(mine, swap_cores(theirs))
    return jnp.concatenate([left, right], axis=1)


def solution(mesh):
    wide, narrow = mesh.shape["wide"], mesh.shape["narrow"]
    near = math.gcd(narrow, 2)
    finer = Mesh(mesh.devices.reshape(wide // 2, 2, narrow // near, near), ALL)
    placed = (
        P(ALL, None),
        P(ALL, None, None),
        P(ALL, None, None),
        P(),
        P(ALL, None),
        P(),
        P(),
    )
    return jax.shard_map(local, mesh=finer, in_specs=placed, out_specs=P(ALL, None), check_vma=False)
```

```python
import functools
import math

import jax
import jax.numpy as jnp
from jax import lax
from jax.experimental import pallas as pl
from jax.experimental.pallas import tpu as pltpu
from jax.sharding import Mesh, PartitionSpec as P

ORDER = 3
OUTER, CORE, FAR, NEAR = "outer", "core", "far", "near"
ALL = (OUTER, CORE, FAR, NEAR)
CHIPS = (OUTER, FAR, NEAR)
MIB = 1024 * 1024
LANES = 128
IN_HBM, IN_VMEM = pl.BlockSpec(memory_space=pltpu.HBM), pl.BlockSpec(memory_space=pltpu.VMEM)
F32, BF16 = jnp.float32, jnp.bfloat16


def whole_block(shape):
    return pl.BlockSpec(shape, lambda *_: (0,) * len(shape))


def kernel_params(mib):
    return pltpu.CompilerParams(vmem_limit_bytes=mib * MIB)


def block_ids(sector_sizes, count):
    ends = jnp.cumsum(sector_sizes)
    ids = jnp.arange(count, dtype=jnp.int32)
    return jnp.sum((ids[:, None] >= ends[None, :]).astype(jnp.int32), axis=1)


def swap_cores(value):
    return lax.ppermute(value, CORE, [(0, 1), (1, 0)])


def partner(position, k, size):
    if size & (size - 1):
        return (position + k) % size
    return position ^ k


def send_round(value, axes, size):
    slots = [value]
    for k in range(1, size):
        slots.append(lax.ppermute(value, axes, [(partner(i, k, size), i) for i in range(size)]))
    return slots


def place_kernel(place_ref, *refs):
    slots, (basis_ref, state_ref) = refs[:-2], refs[-2:]
    outer, _, far, near, _, _ = basis_ref.shape
    half = state_ref.shape[-1]
    across, along, core = place_ref[0], place_ref[1], place_ref[2]
    for j, (own, other) in enumerate(zip(slots[::2], slots[1::2])):
        there = partner(across, j, outer * near)
        o, n = there // near, lax.rem(there, near)
        for k in range(far):
            f = partner(along, k, far)
            for c, slot in ((core, own), (1 - core, other)):
                basis_ref[o, c, f, n, :, :half] = slot[k, 0]
                basis_ref[o, c, f, n, :, half:] = slot[k, 1]
            for c in range(2):
                state_ref[o, f, n, c] = own[k, 2 + c]


def place_slots(place, slots, outer, near):
    far, _, rows, half = slots[0].shape
    basis = ((outer, 2, far, near, rows, 2 * half), BF16)
    state = ((outer, far, near, 2, rows, half), BF16)
    return local_call(place_kernel, "place_slots", 8, basis, state)(place, *slots)


def deal_kernel(right_ref, out_ref, held, in_sems, out_sems):
    pairs, devices = held.shape[:2]
    count = in_sems.shape[1]
    size = devices // count
    places = [(s, g, pl.ds(g * size, size)) for s in range(pairs) for g in range(count)]
    loads = [
        pltpu.make_async_copy(right_ref.at[s, part], held.at[s, part], in_sems.at[s, g])
        for s, g, part in places
    ]
    stores = [
        pltpu.make_async_copy(held.at[s, part], out_ref.at[part, s], out_sems.at[s, g])
        for s, g, part in places
    ]
    for load in loads:
        load.start()
    for load, store in zip(loads, stores):
        load.wait()
        store.start()
    for store in stores:
        store.wait()


def deal_rows(right_ops, devices):
    pairs, states, _ = right_ops.shape
    rows = states // devices
    split = right_ops.reshape(pairs, devices, rows, states)
    if rows % 16:
        return split.transpose(1, 0, 2, 3)
    count = 1
    return pl.pallas_call(
        deal_kernel,
        in_specs=[IN_HBM],
        out_specs=IN_HBM,
        out_shape=jax.ShapeDtypeStruct((devices, pairs, rows, states), BF16),
        scratch_shapes=[
            pltpu.VMEM(split.shape, BF16),
            pltpu.SemaphoreType.DMA((pairs, count)),
            pltpu.SemaphoreType.DMA((pairs, count)),
        ],
        compiler_params=kernel_params(61),
        name="deal_rows",
    )(split)


def build_kernel(basis_ref, left_ref, built_ref):
    basis = basis_ref[...]
    rotated = jnp.dot(left_ref[0], basis, preferred_element_type=F32).astype(BF16)
    built = lax.dot_general(basis, rotated, (((0,), (0,)), ((), ())), preferred_element_type=F32)
    built_ref[0] = built.astype(BF16)


def build(basis, left_ops):
    pairs, states, _ = left_ops.shape
    return pl.pallas_call(
        build_kernel,
        grid=(pairs,),
        in_specs=[
            whole_block((states, states)),
            pl.BlockSpec((1, states, states), lambda s: (s, 0, 0)),
        ],
        out_specs=pl.BlockSpec((1, states, states), lambda s: (s, 0, 0)),
        out_shape=jax.ShapeDtypeStruct(left_ops.shape, BF16),
        compiler_params=kernel_params(60),
        cost_estimate=pl.CostEstimate(flops=0, bytes_accessed=0, transcendentals=0),
        name="build",
    )(basis, left_ops)


def mix_kernel(mixing_ref, right_ref, out_ref, taken, given, mixed, sems):
    total = mixing_ref.shape[0]
    wide, narrow, block, half = mixed.shape[1:]
    rows = right_ref.shape[0] // total
    lanes = half // LANES
    mixing = mixing_ref[...]
    stores = [
        pltpu.make_async_copy(mixed.at[h, w], out_ref.at[w // 2, h, :, w % 2], sems.at[h, w])
        for h in range(2)
        for w in range(wide)
    ]
    for h in range(2):
        places = range(h * lanes, (h + 1) * lanes)
        for place in places:
            taken[place] = right_ref[:, place * LANES : (place + 1) * LANES].astype(F32)
        for row in range(rows):
            every = pl.ds(row, total, stride=rows)
            one = jnp.concatenate([taken[place, every] for place in places], axis=1).astype(BF16)
            one = jnp.dot(mixing, one, preferred_element_type=F32)
            for lane, place in enumerate(places):
                given[place, every] = one[:, lane * LANES : (lane + 1) * LANES]
        for lane, place in enumerate(places):
            done = given[place].astype(BF16).reshape(wide, narrow, block, LANES)
            mixed[h, :, :, :, lane * LANES : (lane + 1) * LANES] = done
        for w in range(wide):
            stores[h * wide + w].start()
    for store in stores:
        store.wait()


def mix(mixing, right_rows, wide, narrow, block):
    size, states = right_rows.shape
    total = mixing.shape[0]
    half = states // 2
    if block % 16:
        mixed = jnp.einsum(
            "st,tx->sx", mixing, right_rows.reshape(total, -1), preferred_element_type=F32
        )
        mixed = mixed.astype(BF16).reshape(wide // 2, 2, narrow, block, 2, half)
        return mixed.transpose(0, 4, 2, 1, 3, 5)
    return pl.pallas_call(
        mix_kernel,
        in_specs=[IN_VMEM, IN_VMEM],
        out_specs=IN_HBM,
        out_shape=jax.ShapeDtypeStruct((wide // 2, 2, narrow, 2, block, half), BF16),
        scratch_shapes=[
            pltpu.VMEM((states // LANES, size, LANES), F32),
            pltpu.VMEM((states // LANES, size, LANES), F32),
            pltpu.VMEM((2, wide, narrow, block, half), BF16),
            pltpu.SemaphoreType.DMA((2, wide)),
        ],
        compiler_params=kernel_params(16),
        cost_estimate=pl.CostEstimate(flops=2 * size * total * states, bytes_accessed=4 * size * states, transcendentals=0),
        name="mix",
    )(mixing, right_rows)


def apply_kernel(state_ref, own_ref, other_ref, applied_ref):
    outer, narrow, _, rows, half = state_ref.shape
    pairs = own_ref.shape[0]
    state = jnp.concatenate(
        [state_ref[y, :, c].reshape(narrow * rows, half) for y in range(outer) for c in range(2)]
    )
    for side, ref in enumerate((own_ref, other_ref)):
        for q in range(pairs):
            one = jnp.dot(ref[q], state, preferred_element_type=F32).astype(BF16)
            column = (side * pairs + q) * half
            applied_ref[:, column : column + half] = one


def store_term(applied, joined, term_ref):
    outer, narrow, _, rows, half = term_ref.shape
    joined = joined.reshape(half, -1)
    term = lax.dot_general(applied, joined, (((1,), (1,)), ((), ())), preferred_element_type=F32)
    term = term.astype(term_ref.dtype).reshape(outer, 2, narrow, rows, half)
    for c in range(2):
        term_ref[:, :, c] = term[:, c]


def join_kernel(core_ref, applied_ref, comp_ref, keep_ref, send_ref, joined_ref):
    outer, narrow, _, rows, half = keep_ref.shape
    pairs = comp_ref.shape[1] // 2
    chips = outer * narrow
    core = core_ref[0]
    for k, (place, term_ref) in enumerate(((1 - core, send_ref), (core, keep_ref))):
        for n in range(2 * pairs):
            pair = n + pairs * (core if n < pairs else -core)
            joined_ref[k, :, :, n * half : (n + 1) * half] = comp_ref[pl.ds(place * chips, chips), pair]
        store_term(applied_ref[...], joined_ref[k], term_ref)


def apply_term_kernel(state_ref, own_ref, other_ref, joined_ref, keep_ref, send_ref, applied_ref):
    apply_kernel(state_ref, own_ref, other_ref, applied_ref)
    for k, term_ref in enumerate((send_ref, keep_ref)):
        store_term(applied_ref[...], joined_ref[k], term_ref)


def local_call(kernel, name, mib, *out, scratch=(), flops=0):
    def call(*operands):
        specs = [
            pl.BlockSpec(memory_space=pltpu.SMEM) if value.dtype == jnp.int32 else IN_VMEM
            for value in operands
        ]
        return pl.pallas_call(
            kernel,
            in_specs=specs,
            out_specs=[IN_VMEM] * len(out),
            out_shape=[jax.ShapeDtypeStruct(*one) for one in out],
            scratch_shapes=scratch,
            compiler_params=kernel_params(mib),
            cost_estimate=pl.CostEstimate(
                flops=flops, bytes_accessed=sum(2 * value.size for value in operands if flops), transcendentals=0
            ),
            name=name,
        )(*operands)

    return call


def apply_pairs(state, own, other):
    outer, narrow, _, rows, half = state.shape
    pairs, states, _ = own.shape
    if rows % 16:
        full = state.transpose(0, 2, 1, 3, 4).reshape(states, half)
        built = jnp.concatenate([own, other])
        applied = jnp.einsum("sil,lk->isk", built, full, preferred_element_type=F32).astype(BF16)
        return applied.reshape(states, 2 * pairs * half)
    shape = (states, 2 * pairs * half)
    return local_call(apply_kernel, "apply_pairs", 8, (shape, BF16))(state, own, other)[0]


def join_terms(core, applied, comp, outer, narrow):
    devices, both, rows, half = comp.shape
    states = devices * rows
    if rows % 16:
        split = comp.reshape(2, devices // 2, 2, both // 2, rows, half)
        split = jnp.stack([split[1 - core], split[core]])
        split = jnp.concatenate([split[:, :, core], split[:, :, 1 - core]], axis=2)
        joined = split.transpose(0, 1, 3, 2, 4).reshape(2, devices // 2, rows, both * half)
        return *terms_of(applied, joined, outer, narrow), joined
    shape = (outer, narrow, 2, rows, half)
    out = (shape, F32), (shape, BF16), ((2, devices // 2, rows, both * half), BF16)
    flops = 2 * states * applied.size
    call = local_call(join_kernel, "join_terms", 12, *out, flops=flops)
    return call(core.reshape(1), applied, comp)


def terms_of(applied, joined, outer, narrow):
    _, chips, rows, width = joined.shape
    states = 2 * chips * rows
    term = jnp.einsum("ix,kjx->kij", applied, joined.reshape(2, states // 2, width), preferred_element_type=F32)
    term = term.reshape(2, outer, 2, narrow, rows, states // 2).transpose(0, 1, 3, 2, 4, 5)
    return term[1], term[0].astype(BF16)


def apply_and_terms(state, own, other, joined):
    outer, narrow, _, rows, half = state.shape
    pairs, states, _ = own.shape
    if rows % 16:
        return terms_of(apply_pairs(state, own, other), joined, outer, narrow)
    scratch = [pltpu.VMEM((states, 2 * pairs * half), BF16)]
    out = (state.shape, F32), (state.shape, BF16)
    flops = 8 * pairs * states**2 * half
    call = local_call(apply_term_kernel, "apply_terms", 12, *out, scratch=scratch, flops=flops)
    return call(state, own, other, joined)


def local(site_basis, left_ops, right_ops, integrals, wavefunction, pair_order, sector_sizes):
    outer, far, near = (lax.axis_size(name) for name in CHIPS)
    narrow = far * near
    wide = 2 * outer
    devices = wide * narrow
    rows, states = wavefunction.shape
    half = states // 2
    pairs = left_ops.shape[0]
    pair_total = integrals.shape[0]
    chips = outer * narrow
    own_outer, own_core, own_narrow = (lax.axis_index(name) for name in (OUTER, CORE, (FAR, NEAR)))
    is_high = own_core == 1

    def own_half(value):
        return jnp.where(is_high, value[..., half:], value[..., :half])

    def other_half(value):
        return jnp.where(is_high, value[..., :half], value[..., half:])

    def by_core(own, other):
        return jnp.stack([jnp.where(is_high, other, own), jnp.where(is_high, own, other)])

    parts = deal_rows(right_ops, devices).reshape(devices, pairs * rows, states)
    parts, wavefunction, site_basis = lax.optimization_barrier((parts, wavefunction, site_basis))
    right_rows = lax.all_to_all(parts, ALL, split_axis=0, concat_axis=0, tiled=True)
    right_rows = right_rows.reshape(pair_total * rows, states)
    mixing = jnp.take(jnp.take(integrals, pair_order, axis=0), pair_order, axis=1)

    blocks = block_ids(sector_sizes, states).astype(F32)
    by_device = blocks.reshape(outer, 2, narrow, rows)
    chip_rows = lax.dynamic_slice(by_device, (own_outer, 0, own_narrow, 0), (1, 2, 1, rows)).reshape(2, rows)
    own_columns = own_half(blocks)
    local_mask = (jnp.abs(chip_rows[:, :, None] - own_columns[None, None, :]) <= 2.0).astype(F32)

    piece = by_core(own_half(wavefunction), swap_cores(other_half(wavefunction)))
    piece = (piece.astype(F32) * local_mask).astype(BF16)
    summed = piece.astype(F32)

    halves = jnp.stack([site_basis[:, :half], site_basis[:, half:]])
    packet = jnp.concatenate([halves, piece])
    packet, local_mask, summed = lax.optimization_barrier((packet, local_mask, summed))
    mixed = mix(mixing, right_rows, wide, narrow, pairs * rows)
    packets, mixed = lax.optimization_barrier((jnp.stack(send_round(packet, FAR, far)), mixed))
    slots = []
    for slot in send_round(packets, (OUTER, NEAR), outer * near):
        slots += [slot, swap_cores(slot[:, :2])]
    place = [lax.axis_index((OUTER, NEAR)), lax.axis_index(FAR), own_core]
    basis, state = place_slots(jnp.stack(place), slots, outer, near)
    state = state.reshape(outer, narrow, 2, rows, half)
    own_built = build(basis.reshape(states, states), left_ops)
    other_built = swap_cores(own_built)
    applied = apply_pairs(state, own_built, other_built)

    mixed = mixed.reshape(devices, 2 * pairs * rows, half)
    comp = lax.all_to_all(mixed, ALL, split_axis=0, concat_axis=0, tiled=True)
    comp = comp.reshape(devices, 2 * pairs, rows, half)

    step_size = 2.0 / math.sqrt(pair_total)
    for order_index in range(1, ORDER + 1):
        if order_index == 1:
            keep, send, joined = join_terms(own_core, applied, comp, outer, narrow)
        else:
            keep, send = apply_and_terms(state, own_built, other_built, joined)
        partial = (keep + swap_cores(send).astype(F32)).astype(BF16)
        partial = partial.reshape(chips, 2 * rows, half)
        arrived = lax.all_to_all(partial, CHIPS, split_axis=0, concat_axis=0, tiled=True)
        term = jnp.sum(arrived.astype(F32), axis=0).reshape(2, rows, half)
        piece = (-(step_size / order_index) * local_mask * term).astype(BF16)
        summed = summed + piece.astype(F32)
        if order_index < ORDER:
            copies = jnp.broadcast_to(piece.reshape(1, 2 * rows, half), (chips, 2 * rows, half))
            state = lax.all_to_all(copies, CHIPS, split_axis=0, concat_axis=0, tiled=True)
            state = state.reshape(outer, narrow, 2, rows, half)

    mine = jnp.where(is_high, summed[1], summed[0])
    theirs = jnp.where(is_high, summed[0], summed[1])
    left, right = by_core(mine, swap_cores(theirs))
    return jnp.concatenate([left, right], axis=1)


def solution(mesh):
    wide, narrow = mesh.shape["wide"], mesh.shape["narrow"]
    near = math.gcd(narrow, 2)
    finer = Mesh(mesh.devices.reshape(wide // 2, 2, narrow // near, near), ALL)
    placed = (
        P(ALL, None),
        P(ALL, None, None),
        P(ALL, None, None),
        P(),
        P(ALL, None),
        P(),
        P(),
    )
    return jax.shard_map(local, mesh=finer, in_specs=placed, out_specs=P(ALL, None), check_vma=False)
```

```python
import functools
import itertools
import math

import jax
import jax.numpy as jnp
from jax import lax
from jax.experimental import pallas as pl
from jax.experimental.pallas import tpu as pltpu
from jax.sharding import Mesh, PartitionSpec as P

ORDER = 3
OUTER, CORE, HIGH, LOW, NEAR = "outer", "core", "high", "low", "near"
ALL = (OUTER, CORE, HIGH, LOW, NEAR)
CHIPS = (OUTER, HIGH, LOW, NEAR)
CUBE = (OUTER, LOW, NEAR)
MIB = 1024 * 1024
LANES = 128
IN_HBM, IN_VMEM = pl.BlockSpec(memory_space=pltpu.HBM), pl.BlockSpec(memory_space=pltpu.VMEM)
F32, BF16 = jnp.float32, jnp.bfloat16


def whole_block(shape):
    return pl.BlockSpec(shape, lambda *_: (0,) * len(shape))


def kernel_params(mib):
    return pltpu.CompilerParams(vmem_limit_bytes=mib * MIB)


def block_ids(sector_sizes, count):
    ends = jnp.cumsum(sector_sizes)
    ids = jnp.arange(count, dtype=jnp.int32)
    return jnp.sum((ids[:, None] >= ends[None, :]).astype(jnp.int32), axis=1)


def swap_cores(value):
    return lax.ppermute(value, CORE, [(0, 1), (1, 0)])


def add_high(value):
    if lax.axis_size(HIGH) == 1:
        return value
    rounded = value.astype(BF16)
    other = lax.ppermute(rounded, HIGH, [(0, 1), (1, 0)])
    return rounded.astype(F32) + other.astype(F32)


def partner(position, k, size):
    if size & (size - 1):
        return (position + k) % size
    return position ^ k


def send_round(value, axes, size):
    slots = [value]
    for k in range(1, size):
        slots.append(lax.ppermute(value, axes, [(partner(i, k, size), i) for i in range(size)]))
    return slots


def place_kernel(place_ref, *refs):
    slots, (basis_ref, state_ref) = refs[:-2], refs[-2:]
    outer, _, far, near, _, _ = basis_ref.shape
    low = state_ref.shape[1] // near
    half = state_ref.shape[-1]
    across, along, core = place_ref[0], place_ref[1], place_ref[2]
    for j, (own, other) in enumerate(zip(slots[::2], slots[1::2])):
        there = partner(across, j, outer * near)
        o, n = there // near, lax.rem(there, near)
        for k in range(far):
            f = partner(along, k, far)
            for c, slot in ((core, own), (1 - core, other)):
                basis_ref[o, c, f, n, :, :half] = slot[k, 0]
                basis_ref[o, c, f, n, :, half:] = slot[k, 1]
            for c in range(2):
                state_ref[o, lax.rem(f, low) * near + n, f // low, c] = own[k, 2 + c]


def place_slots(place, slots, outer, high, near):
    far, _, rows, half = slots[0].shape
    basis = ((outer, 2, far, near, rows, 2 * half), BF16)
    state = ((outer, far // high * near, high, 2, rows, half), BF16)
    return local_call(place_kernel, "place_slots", 8, basis, state)(place, *slots)


def deal_kernel(right_ref, out_ref, held, in_sems, out_sems):
    pairs, devices = held.shape[:2]
    count = in_sems.shape[1]
    size = devices // count
    places = [(s, g, pl.ds(g * size, size)) for s in range(pairs) for g in range(count)]
    loads = [
        pltpu.make_async_copy(right_ref.at[s, part], held.at[s, part], in_sems.at[s, g])
        for s, g, part in places
    ]
    stores = [
        pltpu.make_async_copy(held.at[s, part], out_ref.at[part, s], out_sems.at[s, g])
        for s, g, part in places
    ]
    for load in loads:
        load.start()
    for load, store in zip(loads, stores):
        load.wait()
        store.start()
    for store in stores:
        store.wait()


def deal_rows(right_ops, devices):
    pairs, states, _ = right_ops.shape
    rows = states // devices
    split = right_ops.reshape(pairs, devices, rows, states)
    if rows % 16:
        return split.transpose(1, 0, 2, 3)
    count = 1
    return pl.pallas_call(
        deal_kernel,
        in_specs=[IN_HBM],
        out_specs=IN_HBM,
        out_shape=jax.ShapeDtypeStruct((devices, pairs, rows, states), BF16),
        scratch_shapes=[
            pltpu.VMEM(split.shape, BF16),
            pltpu.SemaphoreType.DMA((pairs, count)),
            pltpu.SemaphoreType.DMA((pairs, count)),
        ],
        compiler_params=kernel_params(61),
        name="deal_rows",
    )(split)


def build_kernel(basis_ref, left_ref, built_ref):
    basis = basis_ref[...]
    rotated = jnp.dot(left_ref[0], basis, preferred_element_type=F32).astype(BF16)
    built = lax.dot_general(basis, rotated, (((0,), (0,)), ((), ())), preferred_element_type=F32)
    built_ref[0] = built.astype(BF16)


def build(basis, left_ops):
    pairs, states, _ = left_ops.shape
    return pl.pallas_call(
        build_kernel,
        grid=(pairs,),
        in_specs=[
            whole_block((states, states)),
            pl.BlockSpec((1, states, states), lambda s: (s, 0, 0)),
        ],
        out_specs=pl.BlockSpec((1, states, states), lambda s: (s, 0, 0)),
        out_shape=jax.ShapeDtypeStruct(left_ops.shape, BF16),
        compiler_params=kernel_params(60),
        cost_estimate=pl.CostEstimate(flops=0, bytes_accessed=0, transcendentals=0),
        name="build",
    )(basis, left_ops)


def mix_kernel(mixing_ref, right_ref, out_ref, taken, given, mixed, sems):
    total = mixing_ref.shape[0]
    wide, narrow, block, half = mixed.shape[1:]
    rows = right_ref.shape[0] // total
    lanes = half // LANES
    mixing = mixing_ref[...]
    stores = [
        pltpu.make_async_copy(mixed.at[h, w], out_ref.at[w // 2, h, :, w % 2], sems.at[h, w])
        for h in range(2)
        for w in range(wide)
    ]
    for h in range(2):
        places = range(h * lanes, (h + 1) * lanes)
        for place in places:
            taken[place] = right_ref[:, place * LANES : (place + 1) * LANES].astype(F32)
        for row in range(rows):
            every = pl.ds(row, total, stride=rows)
            one = jnp.concatenate([taken[place, every] for place in places], axis=1).astype(BF16)
            one = jnp.dot(mixing, one, preferred_element_type=F32)
            for lane, place in enumerate(places):
                given[place, every] = one[:, lane * LANES : (lane + 1) * LANES]
        for lane, place in enumerate(places):
            done = given[place].astype(BF16).reshape(wide, narrow, block, LANES)
            mixed[h, :, :, :, lane * LANES : (lane + 1) * LANES] = done
        for w in range(wide):
            stores[h * wide + w].start()
    for store in stores:
        store.wait()


def mix(mixing, right_rows, wide, narrow, block):
    size, states = right_rows.shape
    total = mixing.shape[0]
    half = states // 2
    if block % 16:
        mixed = jnp.einsum(
            "st,tx->sx", mixing, right_rows.reshape(total, -1), preferred_element_type=F32
        )
        mixed = mixed.astype(BF16).reshape(wide // 2, 2, narrow, block, 2, half)
        return mixed.transpose(0, 4, 2, 1, 3, 5)
    return pl.pallas_call(
        mix_kernel,
        in_specs=[IN_VMEM, IN_VMEM],
        out_specs=IN_HBM,
        out_shape=jax.ShapeDtypeStruct((wide // 2, 2, narrow, 2, block, half), BF16),
        scratch_shapes=[
            pltpu.VMEM((states // LANES, size, LANES), F32),
            pltpu.VMEM((states // LANES, size, LANES), F32),
            pltpu.VMEM((2, wide, narrow, block, half), BF16),
            pltpu.SemaphoreType.DMA((2, wide)),
        ],
        compiler_params=kernel_params(16),
        cost_estimate=pl.CostEstimate(flops=2 * size * total * states, bytes_accessed=4 * size * states, transcendentals=0),
        name="mix",
    )(mixing, right_rows)


def apply_kernel(state_ref, own_ref, other_ref, applied_ref):
    outer, cube, high, _, rows, half = state_ref.shape
    pairs = own_ref.shape[0]
    places = itertools.product(range(outer), range(2), range(high))
    state = jnp.concatenate(
        [state_ref[o, :, h, c].reshape(cube * rows, half) for o, c, h in places]
    )
    for side, ref in enumerate((own_ref, other_ref)):
        for q in range(pairs):
            one = jnp.dot(ref[q], state, preferred_element_type=F32).astype(BF16)
            column = (side * pairs + q) * half
            applied_ref[:, column : column + half] = one


def term_shape(state_shape, last):
    outer, cube, high, _, rows, half = state_shape
    return (outer, high, cube, 2, rows, half) if last else state_shape


def store_term(last, applied, joined, term_ref):
    outer, cube, high, _, rows, half = term_ref.shape
    if last:
        high, cube = cube, high
    joined = joined.reshape(half, -1)
    term = lax.dot_general(applied, joined, (((1,), (1,)), ((), ())), preferred_element_type=F32)
    term = term.astype(term_ref.dtype).reshape(outer, 2, high, cube, rows, half)
    for c in range(2):
        for h in range(high):
            if last:
                term_ref[:, h, :, c] = term[:, c, h]
            else:
                term_ref[:, :, h, c] = term[:, c, h]


def join_kernel(core_ref, applied_ref, comp_ref, keep_ref, send_ref, joined_ref):
    half = keep_ref.shape[-1]
    chips, pairs = comp_ref.shape[0] // 2, comp_ref.shape[1] // 2
    core = core_ref[0]
    for k, (place, term_ref) in enumerate(((1 - core, send_ref), (core, keep_ref))):
        for n in range(2 * pairs):
            pair = n + pairs * (core if n < pairs else -core)
            joined_ref[k, :, :, n * half : (n + 1) * half] = comp_ref[pl.ds(place * chips, chips), pair]
        store_term(False, applied_ref[...], joined_ref[k], term_ref)


def apply_term_kernel(last, state_ref, own_ref, other_ref, joined_ref, keep_ref, send_ref, applied_ref):
    apply_kernel(state_ref, own_ref, other_ref, applied_ref)
    for k, term_ref in enumerate((send_ref, keep_ref)):
        store_term(last, applied_ref[...], joined_ref[k], term_ref)


def local_call(kernel, name, mib, *out, scratch=(), flops=0):
    def call(*operands):
        specs = [
            pl.BlockSpec(memory_space=pltpu.SMEM) if value.dtype == jnp.int32 else IN_VMEM
            for value in operands
        ]
        return pl.pallas_call(
            kernel,
            in_specs=specs,
            out_specs=[IN_VMEM] * len(out),
            out_shape=[jax.ShapeDtypeStruct(*one) for one in out],
            scratch_shapes=scratch,
            compiler_params=kernel_params(mib),
            cost_estimate=pl.CostEstimate(
                flops=flops, bytes_accessed=sum(2 * value.size for value in operands if flops), transcendentals=0
            ),
            name=name,
        )(*operands)

    return call


def apply_pairs(state, own, other):
    pairs, states, _ = own.shape
    half = state.shape[-1]
    if state.shape[-2] % 16:
        full = state.transpose(0, 3, 2, 1, 4, 5).reshape(states, half)
        built = jnp.concatenate([own, other])
        applied = jnp.einsum("sil,lk->isk", built, full, preferred_element_type=F32).astype(BF16)
        return applied.reshape(states, 2 * pairs * half)
    shape = (states, 2 * pairs * half)
    return local_call(apply_kernel, "apply_pairs", 8, (shape, BF16))(state, own, other)[0]


def join_terms(core, applied, comp, shape):
    devices, both, rows, half = comp.shape
    if rows % 16:
        split = comp.reshape(2, devices // 2, 2, both // 2, rows, half)
        split = jnp.stack([split[1 - core], split[core]])
        split = jnp.concatenate([split[:, :, core], split[:, :, 1 - core]], axis=2)
        joined = split.transpose(0, 1, 3, 2, 4).reshape(2, devices // 2, rows, both * half)
        return *terms_of(applied, joined, shape, False), joined
    out = (shape, F32), (shape, BF16), ((2, devices // 2, rows, both * half), BF16)
    flops = 2 * devices * rows * applied.size
    call = local_call(join_kernel, "join_terms", 12, *out, flops=flops)
    return call(core.reshape(1), applied, comp)


def terms_of(applied, joined, shape, last):
    outer, cube, high, _, rows, half = shape
    joined = joined.reshape(2, half, -1)
    term = jnp.einsum("ix,kjx->kij", applied, joined, preferred_element_type=F32)
    term = term.reshape(2, outer, 2, high, cube, rows, half)
    term = term.transpose((0, 1, 3, 4, 2, 5, 6) if last else (0, 1, 4, 3, 2, 5, 6))
    return term[1], term[0].astype(BF16)


def apply_and_terms(state, own, other, joined, last):
    pairs, states, _ = own.shape
    half = state.shape[-1]
    if state.shape[-2] % 16:
        return terms_of(apply_pairs(state, own, other), joined, state.shape, last)
    scratch = [pltpu.VMEM((states, 2 * pairs * half), BF16)]
    shape = term_shape(state.shape, last)
    flops = 8 * pairs * states**2 * half
    kernel = functools.partial(apply_term_kernel, last)
    call = local_call(kernel, "apply_terms", 12, (shape, F32), (shape, BF16), scratch=scratch, flops=flops)
    return call(state, own, other, joined)


def local(site_basis, left_ops, right_ops, integrals, wavefunction, pair_order, sector_sizes):
    outer, high, low, near = (lax.axis_size(name) for name in CHIPS)
    narrow = high * low * near
    wide = 2 * outer
    devices = wide * narrow
    rows, states = wavefunction.shape
    half = states // 2
    pairs = left_ops.shape[0]
    pair_total = integrals.shape[0]
    chips = outer * narrow
    own_core, own_high = lax.axis_index(CORE), lax.axis_index(HIGH)
    is_high = own_core == 1

    def own_half(value):
        return jnp.where(is_high, value[..., half:], value[..., :half])

    def other_half(value):
        return jnp.where(is_high, value[..., :half], value[..., half:])

    def by_core(own, other):
        return jnp.stack([jnp.where(is_high, other, own), jnp.where(is_high, own, other)])

    parts = deal_rows(right_ops, devices).reshape(devices, pairs * rows, states)
    parts, wavefunction, site_basis = lax.optimization_barrier((parts, wavefunction, site_basis))
    right_rows = lax.all_to_all(parts, ALL, split_axis=0, concat_axis=0, tiled=True)
    right_rows = right_rows.reshape(pair_total * rows, states)
    mixing = jnp.take(jnp.take(integrals, pair_order, axis=0), pair_order, axis=1)

    blocks = block_ids(sector_sizes, states).astype(F32)
    by_device = blocks.reshape(outer, 2, high, low, near, rows)
    first = (lax.axis_index(OUTER), 0, 0, lax.axis_index(LOW), lax.axis_index(NEAR), 0)
    cube_rows = lax.dynamic_slice(by_device, first, (1, 2, high, 1, 1, rows))
    cube_rows = cube_rows.reshape(2, high, rows).transpose(1, 0, 2)
    own_columns = own_half(blocks)
    cube_mask = (jnp.abs(cube_rows[..., None] - own_columns) <= 2.0).astype(F32)
    local_mask = lax.dynamic_index_in_dim(cube_mask, own_high, 0, keepdims=False)

    piece = by_core(own_half(wavefunction), swap_cores(other_half(wavefunction)))
    piece = (piece.astype(F32) * local_mask).astype(BF16)
    summed = piece.astype(F32)

    halves = jnp.stack([site_basis[:, :half], site_basis[:, half:]])
    packet = jnp.concatenate([halves, piece])
    packet, local_mask, cube_mask, summed = lax.optimization_barrier(
        (packet, local_mask, cube_mask, summed)
    )
    mixed = mix(mixing, right_rows, wide, narrow, pairs * rows)
    packets, mixed = lax.optimization_barrier((jnp.stack(send_round(packet, (HIGH, LOW), high * low)), mixed))
    slots = []
    for slot in send_round(packets, (OUTER, NEAR), outer * near):
        slots += [slot, swap_cores(slot[:, :2])]
    place = [lax.axis_index((OUTER, NEAR)), lax.axis_index((HIGH, LOW)), own_core]
    basis, state = place_slots(jnp.stack(place), slots, outer, high, near)
    own_built = build(basis.reshape(states, states), left_ops)
    other_built = swap_cores(own_built)
    applied = apply_pairs(state, own_built, other_built)

    mixed = mixed.reshape(devices, 2 * pairs * rows, half)
    comp = lax.all_to_all(mixed, ALL, split_axis=0, concat_axis=0, tiled=True)
    comp = comp.reshape(devices, 2 * pairs, rows, half)

    step_size = 2.0 / math.sqrt(pair_total)
    for order_index in range(1, ORDER + 1):
        last = order_index == ORDER
        if order_index == 1:
            keep, send, joined = join_terms(own_core, applied, comp, state.shape)
        else:
            keep, send = apply_and_terms(state, own_built, other_built, joined, last)
        partial = (keep + swap_cores(send).astype(F32)).astype(BF16)
        factor = -(step_size / order_index)
        if last:
            partial = partial.reshape(chips, 2 * rows, half)
            arrived = lax.all_to_all(partial, CHIPS, split_axis=0, concat_axis=0, tiled=True)
            term = jnp.sum(arrived.astype(F32), axis=0).reshape(2, rows, half)
            piece = (factor * local_mask * term).astype(BF16)
        else:
            partial = partial.reshape(chips // high, high * 2 * rows, half)
            arrived = lax.all_to_all(partial, CUBE, split_axis=0, concat_axis=0, tiled=True)
            term = jnp.sum(arrived.astype(F32), axis=0).reshape(cube_mask.shape)
            term = add_high(cube_mask * term)
            pieces = (factor * cube_mask * term).astype(BF16)
            piece = lax.dynamic_index_in_dim(pieces, own_high, 0, keepdims=False)
            copies = jnp.broadcast_to(pieces.reshape(partial.shape[1:]), partial.shape)
            state = lax.all_to_all(copies, CUBE, split_axis=0, concat_axis=0, tiled=True)
            state = state.reshape(outer, low * near, high, 2, rows, half)
        summed = summed + piece.astype(F32)

    mine = jnp.where(is_high, summed[1], summed[0])
    theirs = jnp.where(is_high, summed[0], summed[1])
    left, right = by_core(mine, swap_cores(theirs))
    return jnp.concatenate([left, right], axis=1)


def solution(mesh):
    wide, narrow = mesh.shape["wide"], mesh.shape["narrow"]
    near = math.gcd(narrow, 2)
    high = math.gcd(narrow // near, 2)
    finer = Mesh(mesh.devices.reshape(wide // 2, 2, high, narrow // near // high, near), ALL)
    placed = (
        P(ALL, None),
        P(ALL, None, None),
        P(ALL, None, None),
        P(),
        P(ALL, None),
        P(),
        P(),
    )
    return jax.shard_map(local, mesh=finer, in_specs=placed, out_specs=P(ALL, None), check_vma=False)
```

```python
import functools
import itertools
import math

import jax
import jax.numpy as jnp
from jax import lax
from jax.experimental import pallas as pl
from jax.experimental.pallas import tpu as pltpu
from jax.sharding import Mesh, PartitionSpec as P

ORDER = 3
OUTER, CORE, HIGH, LOW, NEAR = "outer", "core", "high", "low", "near"
ALL = (OUTER, CORE, HIGH, LOW, NEAR)
CHIPS = (OUTER, HIGH, LOW, NEAR)
CUBE = (OUTER, LOW, NEAR)
MIB = 1024 * 1024
LANES = 128
IN_HBM, IN_VMEM = pl.BlockSpec(memory_space=pltpu.HBM), pl.BlockSpec(memory_space=pltpu.VMEM)
F32, BF16 = jnp.float32, jnp.bfloat16


def whole_block(shape):
    return pl.BlockSpec(shape, lambda *_: (0,) * len(shape))


def kernel_params(mib):
    return pltpu.CompilerParams(vmem_limit_bytes=mib * MIB)


def block_ids(sector_sizes, count):
    ends = jnp.cumsum(sector_sizes)
    ids = jnp.arange(count, dtype=jnp.int32)
    return jnp.sum((ids[:, None] >= ends[None, :]).astype(jnp.int32), axis=1)


def swap_cores(value):
    return lax.ppermute(value, CORE, [(0, 1), (1, 0)])


def add_high(value):
    if lax.axis_size(HIGH) == 1:
        return value
    rounded = value.astype(BF16)
    other = lax.ppermute(rounded, HIGH, [(0, 1), (1, 0)])
    return rounded.astype(F32) + other.astype(F32)


def partner(position, k, size):
    if size & (size - 1):
        return (position + k) % size
    return position ^ k


def send_round(value, axes, size):
    slots = [value]
    for k in range(1, size):
        slots.append(lax.ppermute(value, axes, [(partner(i, k, size), i) for i in range(size)]))
    return slots


def place_kernel(place_ref, *refs):
    slots, (basis_ref, state_ref) = refs[:-2], refs[-2:]
    outer, _, far, near, _, _ = basis_ref.shape
    low = state_ref.shape[1] // near
    half = state_ref.shape[-1]
    across, along, core = place_ref[0], place_ref[1], place_ref[2]
    for j, (own, other) in enumerate(zip(slots[::2], slots[1::2])):
        there = partner(across, j, outer * near)
        o, n = there // near, lax.rem(there, near)
        for k in range(far):
            f = partner(along, k, far)
            for c, slot in ((core, own), (1 - core, other)):
                basis_ref[o, c, f, n, :, :half] = slot[k, 0]
                basis_ref[o, c, f, n, :, half:] = slot[k, 1]
            for c in range(2):
                state_ref[o, lax.rem(f, low) * near + n, f // low, c] = own[k, 2 + c]


def place_slots(place, slots, outer, high, near):
    far, _, rows, half = slots[0].shape
    basis = ((outer, 2, far, near, rows, 2 * half), BF16)
    state = ((outer, far // high * near, high, 2, rows, half), BF16)
    return local_call(place_kernel, "place_slots", 8, basis, state)(place, *slots)


def deal_kernel(right_ref, out_ref, held, in_sems, out_sems):
    pairs, devices = held.shape[:2]
    count = in_sems.shape[1]
    size = devices // count
    places = [(s, g, pl.ds(g * size, size)) for s in range(pairs) for g in range(count)]
    loads = [
        pltpu.make_async_copy(right_ref.at[s, part], held.at[s, part], in_sems.at[s, g])
        for s, g, part in places
    ]
    stores = [
        pltpu.make_async_copy(held.at[s, part], out_ref.at[part, s], out_sems.at[s, g])
        for s, g, part in places
    ]
    for load in loads:
        load.start()
    for load, store in zip(loads, stores):
        load.wait()
        store.start()
    for store in stores:
        store.wait()


def deal_rows(right_ops, devices):
    pairs, states, _ = right_ops.shape
    rows = states // devices
    split = right_ops.reshape(pairs, devices, rows, states)
    if rows % 16:
        return split.transpose(1, 0, 2, 3)
    count = 1
    return pl.pallas_call(
        deal_kernel,
        in_specs=[IN_HBM],
        out_specs=IN_HBM,
        out_shape=jax.ShapeDtypeStruct((devices, pairs, rows, states), BF16),
        scratch_shapes=[
            pltpu.VMEM(split.shape, BF16),
            pltpu.SemaphoreType.DMA((pairs, count)),
            pltpu.SemaphoreType.DMA((pairs, count)),
        ],
        compiler_params=kernel_params(61),
        name="deal_rows",
    )(split)


def build_kernel(basis_ref, left_ref, built_ref):
    basis = basis_ref[...]
    rotated = jnp.dot(left_ref[0], basis, preferred_element_type=F32).astype(BF16)
    built = lax.dot_general(basis, rotated, (((0,), (0,)), ((), ())), preferred_element_type=F32)
    built_ref[0] = built.astype(BF16)


def build(basis, left_ops):
    pairs, states, _ = left_ops.shape
    return pl.pallas_call(
        build_kernel,
        grid=(pairs,),
        in_specs=[
            whole_block((states, states)),
            pl.BlockSpec((1, states, states), lambda s: (s, 0, 0)),
        ],
        out_specs=pl.BlockSpec((1, states, states), lambda s: (s, 0, 0)),
        out_shape=jax.ShapeDtypeStruct(left_ops.shape, BF16),
        compiler_params=kernel_params(60),
        cost_estimate=pl.CostEstimate(flops=0, bytes_accessed=0, transcendentals=0),
        name="build",
    )(basis, left_ops)


def mix_kernel(mixing_ref, right_ref, out_ref, taken, given, mixed, sems):
    total = mixing_ref.shape[0]
    wide, narrow, block, half = mixed.shape[1:]
    rows = right_ref.shape[0] // total
    lanes = half // LANES
    pitch = taken.shape[2]
    mixing = mixing_ref[...]
    stores = [
        pltpu.make_async_copy(mixed.at[h, w], out_ref.at[w // 2, h, :, w % 2], sems.at[h, w])
        for h in range(2)
        for w in range(wide)
    ]
    for h in range(2):
        places = range(h * lanes, (h + 1) * lanes)
        for place in places:
            part = right_ref[:, place * LANES : (place + 1) * LANES].astype(F32)
            taken[place, :, :rows] = part.reshape(total, rows, LANES)
        flat_in = [taken.at[place].reshape(total * pitch, LANES) for place in places]
        flat_out = [given.at[place].reshape(total * pitch, LANES) for place in places]
        for row in range(rows):
            every = pl.ds(row, total, stride=pitch)
            one = jnp.concatenate([ref[every] for ref in flat_in], axis=1).astype(BF16)
            one = jnp.dot(mixing, one, preferred_element_type=F32)
            for lane, ref in enumerate(flat_out):
                ref[every] = one[:, lane * LANES : (lane + 1) * LANES]
        for lane, place in enumerate(places):
            done = given[place, :, :rows].astype(BF16).reshape(wide, narrow, block, LANES)
            mixed[h, :, :, :, lane * LANES : (lane + 1) * LANES] = done
        for w in range(wide):
            stores[h * wide + w].start()
    for store in stores:
        store.wait()


def mix(mixing, right_rows, wide, narrow, block):
    size, states = right_rows.shape
    total = mixing.shape[0]
    half = states // 2
    if block % 16:
        mixed = jnp.einsum(
            "st,tx->sx", mixing, right_rows.reshape(total, -1), preferred_element_type=F32
        )
        mixed = mixed.astype(BF16).reshape(wide // 2, 2, narrow, block, 2, half)
        return mixed.transpose(0, 4, 2, 1, 3, 5)
    return pl.pallas_call(
        mix_kernel,
        in_specs=[IN_VMEM, IN_VMEM],
        out_specs=IN_HBM,
        out_shape=jax.ShapeDtypeStruct((wide // 2, 2, narrow, 2, block, half), BF16),
        scratch_shapes=[
            pltpu.VMEM((states // LANES, total, size // total + 8, LANES), F32),
            pltpu.VMEM((states // LANES, total, size // total + 8, LANES), F32),
            pltpu.VMEM((2, wide, narrow, block, half), BF16),
            pltpu.SemaphoreType.DMA((2, wide)),
        ],
        compiler_params=kernel_params(16),
        cost_estimate=pl.CostEstimate(flops=2 * size * total * states, bytes_accessed=4 * size * states, transcendentals=0),
        name="mix",
    )(mixing, right_rows)


def apply_kernel(state_ref, own_ref, other_ref, applied_ref):
    outer, cube, high, _, rows, half = state_ref.shape
    pairs = own_ref.shape[0]
    places = itertools.product(range(outer), range(2), range(high))
    state = jnp.concatenate(
        [state_ref[o, :, h, c].reshape(cube * rows, half) for o, c, h in places]
    )
    for side, ref in enumerate((own_ref, other_ref)):
        for q in range(pairs):
            one = jnp.dot(ref[q], state, preferred_element_type=F32).astype(BF16)
            column = (side * pairs + q) * half
            applied_ref[:, column : column + half] = one


def store_term(applied, joined, term_ref):
    outer, cube, high, _, rows, half = term_ref.shape
    joined = joined.reshape(half, -1)
    term = lax.dot_general(applied, joined, (((1,), (1,)), ((), ())), preferred_element_type=F32)
    term = term.astype(term_ref.dtype).reshape(outer, 2, high, cube, rows, half)
    for c in range(2):
        for h in range(high):
            term_ref[:, :, h, c] = term[:, c, h]


def join_kernel(core_ref, applied_ref, comp_ref, keep_ref, send_ref, joined_ref):
    half = keep_ref.shape[-1]
    chips, pairs = comp_ref.shape[0] // 2, comp_ref.shape[1] // 2
    core = core_ref[0]
    for k, (place, term_ref) in enumerate(((1 - core, send_ref), (core, keep_ref))):
        for n in range(2 * pairs):
            pair = n + pairs * (core if n < pairs else -core)
            joined_ref[k, :, :, n * half : (n + 1) * half] = comp_ref[pl.ds(place * chips, chips), pair]
        store_term(applied_ref[...], joined_ref[k], term_ref)


def apply_term_kernel(state_ref, own_ref, other_ref, joined_ref, keep_ref, send_ref, applied_ref):
    apply_kernel(state_ref, own_ref, other_ref, applied_ref)
    for k, term_ref in enumerate((send_ref, keep_ref)):
        store_term(applied_ref[...], joined_ref[k], term_ref)


def last_term_kernel(
    core_ref, state_ref, own_ref, other_ref, joined_ref, keep_ref, send_ref, applied_ref
):
    apply_kernel(state_ref, own_ref, other_ref, applied_ref)
    outer, narrow, _, rows, half = keep_ref.shape
    count = narrow * rows
    core = core_ref[0]
    for c, term_ref in ((1 - core, send_ref), (core, keep_ref)):
        starts = [pl.multiple_of((2 * o + c) * count, count) for o in range(outer)]
        applied = jnp.concatenate([applied_ref[pl.ds(start, count)] for start in starts])
        for k, place in enumerate((1 - core, core)):
            joined = joined_ref[k].reshape(half, -1)
            term = lax.dot_general(applied, joined, (((1,), (1,)), ((), ())), preferred_element_type=F32)
            term = term.astype(term_ref.dtype).reshape(outer, narrow, rows, half)
            term_ref[:, :, place] = term


def local_call(kernel, name, mib, *out, scratch=(), flops=0):
    def call(*operands):
        specs = [
            pl.BlockSpec(memory_space=pltpu.SMEM) if value.dtype == jnp.int32 else IN_VMEM
            for value in operands
        ]
        return pl.pallas_call(
            kernel,
            in_specs=specs,
            out_specs=[IN_VMEM] * len(out),
            out_shape=[jax.ShapeDtypeStruct(*one) for one in out],
            scratch_shapes=scratch,
            compiler_params=kernel_params(mib),
            cost_estimate=pl.CostEstimate(
                flops=flops, bytes_accessed=sum(2 * value.size for value in operands if flops), transcendentals=0
            ),
            name=name,
        )(*operands)

    return call


def apply_pairs(state, own, other):
    pairs, states, _ = own.shape
    half = state.shape[-1]
    if state.shape[-2] % 16:
        full = state.transpose(0, 3, 2, 1, 4, 5).reshape(states, half)
        built = jnp.concatenate([own, other])
        applied = jnp.einsum("sil,lk->isk", built, full, preferred_element_type=F32).astype(BF16)
        return applied.reshape(states, 2 * pairs * half)
    shape = (states, 2 * pairs * half)
    return local_call(apply_kernel, "apply_pairs", 8, (shape, BF16))(state, own, other)[0]


def join_terms(core, applied, comp, shape):
    devices, both, rows, half = comp.shape
    if rows % 16:
        split = comp.reshape(2, devices // 2, 2, both // 2, rows, half)
        split = jnp.stack([split[1 - core], split[core]])
        split = jnp.concatenate([split[:, :, core], split[:, :, 1 - core]], axis=2)
        joined = split.transpose(0, 1, 3, 2, 4).reshape(2, devices // 2, rows, both * half)
        return *terms_of(applied, joined, shape), joined
    out = (shape, F32), (shape, BF16), ((2, devices // 2, rows, both * half), BF16)
    flops = 2 * devices * rows * applied.size
    call = local_call(join_kernel, "join_terms", 12, *out, flops=flops)
    return call(core.reshape(1), applied, comp)


def all_terms(applied, joined, shape):
    outer, cube, high, _, rows, half = shape
    joined = joined.reshape(2, half, -1)
    term = jnp.einsum("ix,kjx->kij", applied, joined, preferred_element_type=F32)
    return term.reshape(2, outer, 2, high, cube, rows, half)


def terms_of(applied, joined, shape):
    term = all_terms(applied, joined, shape).transpose(0, 1, 4, 3, 2, 5, 6)
    return term[1], term[0].astype(BF16)


def apply_and_terms(state, own, other, joined):
    pairs, states, _ = own.shape
    half = state.shape[-1]
    if state.shape[-2] % 16:
        return terms_of(apply_pairs(state, own, other), joined, state.shape)
    scratch = [pltpu.VMEM((states, 2 * pairs * half), BF16)]
    out = (state.shape, F32), (state.shape, BF16)
    flops = 8 * pairs * states**2 * half
    call = local_call(apply_term_kernel, "apply_terms", 12, *out, scratch=scratch, flops=flops)
    return call(state, own, other, joined)


def apply_and_last_terms(core, state, own, other, joined):
    outer, cube, high, _, rows, half = state.shape
    pairs, states, _ = own.shape
    shape = (outer, high * cube, 2, rows, half)
    if rows % 16:
        term = all_terms(apply_pairs(state, own, other), joined, state.shape)
        term = term.reshape(2, outer, 2, high * cube, rows, half)
        term = jnp.where(core == 1, term, term[::-1]).transpose(2, 1, 3, 0, 4, 5)
        return term[core], term[1 - core].astype(BF16)
    scratch = [pltpu.VMEM((states, 2 * pairs * half), BF16)]
    flops = 8 * pairs * states**2 * half
    call = local_call(last_term_kernel, "last_terms", 12, (shape, F32), (shape, BF16), scratch=scratch, flops=flops)
    return call(core.reshape(1), state, own, other, joined)


def local(site_basis, left_ops, right_ops, integrals, wavefunction, pair_order, sector_sizes):
    outer, high, low, near = (lax.axis_size(name) for name in CHIPS)
    narrow = high * low * near
    wide = 2 * outer
    devices = wide * narrow
    rows, states = wavefunction.shape
    half = states // 2
    pairs = left_ops.shape[0]
    pair_total = integrals.shape[0]
    chips = outer * narrow
    own_core, own_high = lax.axis_index(CORE), lax.axis_index(HIGH)
    is_high = own_core == 1

    def own_half(value):
        return jnp.where(is_high, value[..., half:], value[..., :half])

    def other_half(value):
        return jnp.where(is_high, value[..., :half], value[..., half:])

    def by_core(own, other):
        return jnp.stack([jnp.where(is_high, other, own), jnp.where(is_high, own, other)])

    parts = deal_rows(right_ops, devices).reshape(devices, pairs * rows, states)
    parts, wavefunction, site_basis = lax.optimization_barrier((parts, wavefunction, site_basis))
    right_rows = lax.all_to_all(parts, ALL, split_axis=0, concat_axis=0, tiled=True)
    right_rows = right_rows.reshape(pair_total * rows, states)
    mixing = jnp.take(jnp.take(integrals, pair_order, axis=0), pair_order, axis=1)

    blocks = block_ids(sector_sizes, states).astype(F32)
    by_device = blocks.reshape(outer, 2, high, low, near, rows)
    first = (lax.axis_index(OUTER), 0, 0, lax.axis_index(LOW), lax.axis_index(NEAR), 0)
    cube_rows = lax.dynamic_slice(by_device, first, (1, 2, high, 1, 1, rows))
    cube_rows = cube_rows.reshape(2, high, rows).transpose(1, 0, 2)
    own_columns = own_half(blocks)
    cube_mask = (jnp.abs(cube_rows[..., None] - own_columns) <= 2.0).astype(F32)
    local_mask = lax.dynamic_index_in_dim(cube_mask, own_high, 0, keepdims=False)
    own_row = lax.axis_index(ALL) * rows
    own_rows = lax.dynamic_slice_in_dim(blocks, own_row, rows, 0)
    row_mask = (jnp.abs(own_rows[:, None] - blocks.reshape(2, 1, half)) <= 2.0).astype(F32)

    piece = by_core(own_half(wavefunction), swap_cores(other_half(wavefunction)))
    piece = (piece.astype(F32) * local_mask).astype(BF16)
    summed = piece.astype(F32)

    halves = jnp.stack([site_basis[:, :half], site_basis[:, half:]])
    packet = jnp.concatenate([halves, piece])
    packet, cube_mask, row_mask, summed = lax.optimization_barrier(
        (packet, cube_mask, row_mask, summed)
    )
    mixed = mix(mixing, right_rows, wide, narrow, pairs * rows)
    packets, mixed = lax.optimization_barrier((jnp.stack(send_round(packet, (HIGH, LOW), high * low)), mixed))
    slots = []
    for slot in send_round(packets, (OUTER, NEAR), outer * near):
        slots += [slot, swap_cores(slot[:, :2])]
    place = [lax.axis_index((OUTER, NEAR)), lax.axis_index((HIGH, LOW)), own_core]
    basis, state = place_slots(jnp.stack(place), slots, outer, high, near)
    own_built = build(basis.reshape(states, states), left_ops)
    other_built = swap_cores(own_built)
    applied = apply_pairs(state, own_built, other_built)

    mixed = mixed.reshape(devices, 2 * pairs * rows, half)
    comp = lax.all_to_all(mixed, ALL, split_axis=0, concat_axis=0, tiled=True)
    comp = comp.reshape(devices, 2 * pairs, rows, half)

    step_size = 2.0 / math.sqrt(pair_total)
    for order_index in range(1, ORDER):
        if order_index == 1:
            keep, send, joined = join_terms(own_core, applied, comp, state.shape)
        else:
            keep, send = apply_and_terms(state, own_built, other_built, joined)
        partial = (keep + swap_cores(send).astype(F32)).astype(BF16)
        partial = partial.reshape(chips // high, high * 2 * rows, half)
        arrived = lax.all_to_all(partial, CUBE, split_axis=0, concat_axis=0, tiled=True)
        term = jnp.sum(arrived.astype(F32), axis=0).reshape(cube_mask.shape)
        term = add_high(cube_mask * term)
        pieces = (-(step_size / order_index) * cube_mask * term).astype(BF16)
        piece = lax.dynamic_index_in_dim(pieces, own_high, 0, keepdims=False)
        summed = summed + piece.astype(F32)
        copies = jnp.broadcast_to(pieces.reshape(partial.shape[1:]), partial.shape)
        mine = jnp.where(is_high, summed[1], summed[0])
        theirs = jnp.where(is_high, summed[0], summed[1])
        copies, summed, mine, theirs = lax.optimization_barrier((copies, summed, mine, theirs))
        state = lax.all_to_all(copies, CUBE, split_axis=0, concat_axis=0, tiled=True)
        state = state.reshape(outer, low * near, high, 2, rows, half)

    keep, send = apply_and_last_terms(own_core, state, own_built, other_built, joined)
    theirs, send = lax.optimization_barrier((theirs, send))
    theirs, send = lax.optimization_barrier((swap_cores(theirs), swap_cores(send)))
    summed = by_core(mine, theirs)
    partial = (keep + send.astype(F32)).astype(BF16).reshape(chips, 2 * rows, half)
    partial, summed = lax.optimization_barrier((partial, summed))
    arrived = lax.all_to_all(partial, CHIPS, split_axis=0, concat_axis=0, tiled=True)
    term = jnp.sum(arrived.astype(F32), axis=0).reshape(2, rows, half)
    piece = (-(step_size / ORDER) * row_mask * term).astype(BF16)
    summed = summed + piece.astype(F32)
    return jnp.concatenate([summed[0], summed[1]], axis=1)


def solution(mesh):
    wide, narrow = mesh.shape["wide"], mesh.shape["narrow"]
    near = math.gcd(narrow, 2)
    high = math.gcd(narrow // near, 2)
    finer = Mesh(mesh.devices.reshape(wide // 2, 2, high, narrow // near // high, near), ALL)
    placed = (
        P(ALL, None),
        P(ALL, None, None),
        P(ALL, None, None),
        P(),
        P(ALL, None),
        P(),
        P(),
    )
    return jax.shard_map(local, mesh=finer, in_specs=placed, out_specs=P(ALL, None), check_vma=False)
```

```python
import functools
import itertools
import math

import jax
import jax.numpy as jnp
from jax import lax
from jax.experimental import pallas as pl
from jax.experimental.pallas import tpu as pltpu
from jax.sharding import Mesh, PartitionSpec as P

ORDER = 3
OUTER, CORE, HIGH, LOW, NEAR = "outer", "core", "high", "low", "near"
ALL = (OUTER, CORE, HIGH, LOW, NEAR)
CHIPS = (OUTER, HIGH, LOW, NEAR)
CUBE = (OUTER, LOW, NEAR)
MIB = 1024 * 1024
LANES = 128
IN_HBM, IN_VMEM = pl.BlockSpec(memory_space=pltpu.HBM), pl.BlockSpec(memory_space=pltpu.VMEM)
F32, BF16 = jnp.float32, jnp.bfloat16


def whole_block(shape):
    return pl.BlockSpec(shape, lambda *_: (0,) * len(shape))


def kernel_params(mib):
    return pltpu.CompilerParams(vmem_limit_bytes=mib * MIB)


def block_ids(sector_sizes, count):
    ends = jnp.cumsum(sector_sizes)
    ids = jnp.arange(count, dtype=jnp.int32)
    return jnp.sum((ids[:, None] >= ends[None, :]).astype(jnp.int32), axis=1)


def swap_cores(value):
    return lax.ppermute(value, CORE, [(0, 1), (1, 0)])


def add_high(value):
    if lax.axis_size(HIGH) == 1:
        return value
    rounded = value.astype(BF16)
    other = lax.ppermute(rounded, HIGH, [(0, 1), (1, 0)])
    return rounded.astype(F32) + other.astype(F32)


def partner(position, k, size):
    if size & (size - 1):
        return (position + k) % size
    return position ^ k


def send_round(value, axes, size):
    slots = [value]
    for k in range(1, size):
        slots.append(lax.ppermute(value, axes, [(partner(i, k, size), i) for i in range(size)]))
    return slots


def place_kernel(place_ref, *refs):
    slots, (basis_ref, state_ref) = refs[:-2], refs[-2:]
    outer, _, far, near, _, _ = basis_ref.shape
    low = state_ref.shape[1] // near
    half = state_ref.shape[-1]
    across, along, core = place_ref[0], place_ref[1], place_ref[2]
    for j, (own, other) in enumerate(zip(slots[::2], slots[1::2])):
        there = partner(across, j, outer * near)
        o, n = there // near, lax.rem(there, near)
        for k in range(far):
            f = partner(along, k, far)
            for c, slot in ((core, own), (1 - core, other)):
                basis_ref[o, c, f, n, :, :half] = slot[k, 0]
                basis_ref[o, c, f, n, :, half:] = slot[k, 1]
            for c in range(2):
                state_ref[o, lax.rem(f, low) * near + n, f // low, c] = own[k, 2 + c]


def place_slots(place, slots, outer, high, near):
    far, _, rows, half = slots[0].shape
    basis = ((outer, 2, far, near, rows, 2 * half), BF16)
    state = ((outer, far // high * near, high, 2, rows, half), BF16)
    return local_call(place_kernel, "place_slots", 8, basis, state)(place, *slots)


def deal_kernel(right_ref, out_ref, held, in_sems, out_sems):
    pairs, devices = held.shape[:2]
    count = in_sems.shape[1]
    size = devices // count
    places = [(s, g, pl.ds(g * size, size)) for s in range(pairs) for g in range(count)]
    loads = [
        pltpu.make_async_copy(right_ref.at[s, part], held.at[s, part], in_sems.at[s, g])
        for s, g, part in places
    ]
    stores = [
        pltpu.make_async_copy(held.at[s, part], out_ref.at[part, s], out_sems.at[s, g])
        for s, g, part in places
    ]
    for load in loads:
        load.start()
    for load, store in zip(loads, stores):
        load.wait()
        store.start()
    for store in stores:
        store.wait()


def deal_rows(right_ops, devices):
    pairs, states, _ = right_ops.shape
    rows = states // devices
    split = right_ops.reshape(pairs, devices, rows, states)
    if rows % 16:
        return split.transpose(1, 0, 2, 3)
    count = 1
    return pl.pallas_call(
        deal_kernel,
        in_specs=[IN_HBM],
        out_specs=IN_HBM,
        out_shape=jax.ShapeDtypeStruct((devices, pairs, rows, states), BF16),
        scratch_shapes=[
            pltpu.VMEM(split.shape, BF16),
            pltpu.SemaphoreType.DMA((pairs, count)),
            pltpu.SemaphoreType.DMA((pairs, count)),
        ],
        compiler_params=kernel_params(61),
        name="deal_rows",
    )(split)


def build_kernel(basis_ref, left_ref, built_ref):
    basis = basis_ref[...]
    rotated = jnp.dot(left_ref[0], basis, preferred_element_type=F32).astype(BF16)
    built = lax.dot_general(basis, rotated, (((0,), (0,)), ((), ())), preferred_element_type=F32)
    built_ref[0] = built.astype(BF16)


def build(basis, left_ops):
    pairs, states, _ = left_ops.shape
    return pl.pallas_call(
        build_kernel,
        grid=(pairs,),
        in_specs=[
            whole_block((states, states)),
            pl.BlockSpec((1, states, states), lambda s: (s, 0, 0)),
        ],
        out_specs=pl.BlockSpec((1, states, states), lambda s: (s, 0, 0)),
        out_shape=jax.ShapeDtypeStruct(left_ops.shape, BF16),
        compiler_params=kernel_params(60),
        cost_estimate=pl.CostEstimate(flops=0, bytes_accessed=0, transcendentals=0),
        name="build",
    )(basis, left_ops)


def mix_kernel(mixing_ref, right_ref, out_ref, taken, given, mixed, sems):
    total = mixing_ref.shape[0]
    wide, narrow, block, half = mixed.shape[1:]
    rows = right_ref.shape[0] // total
    lanes = half // LANES
    pitch = taken.shape[2]
    mixing = mixing_ref[...]
    stores = [
        pltpu.make_async_copy(mixed.at[h, w], out_ref.at[w // 2, h, :, w % 2], sems.at[h, w])
        for h in range(2)
        for w in range(wide)
    ]
    for h in range(2):
        places = range(h * lanes, (h + 1) * lanes)
        for place in places:
            part = right_ref[:, place * LANES : (place + 1) * LANES].astype(F32)
            taken[place, :total, :rows] = part.reshape(total, rows, LANES)
        flat_in = [taken.at[place].reshape((total + 1) * pitch, LANES) for place in places]
        flat_out = [given.at[place].reshape((total + 1) * pitch, LANES) for place in places]
        for row in range(rows):
            every = pl.ds(row, total, stride=pitch)
            one = jnp.concatenate([ref[every] for ref in flat_in], axis=1).astype(BF16)
            one = jnp.dot(mixing, one, preferred_element_type=F32)
            for lane, ref in enumerate(flat_out):
                ref[every] = one[:, lane * LANES : (lane + 1) * LANES]
        for lane, place in enumerate(places):
            done = given[place, :total, :rows].astype(BF16).reshape(wide, narrow, block, LANES)
            mixed[h, :, :, :, lane * LANES : (lane + 1) * LANES] = done
        for w in range(wide):
            stores[h * wide + w].start()
    for store in stores:
        store.wait()


def mix(mixing, right_rows, wide, narrow, block):
    size, states = right_rows.shape
    total = mixing.shape[0]
    half = states // 2
    if block % 16:
        mixed = jnp.einsum(
            "st,tx->sx", mixing, right_rows.reshape(total, -1), preferred_element_type=F32
        )
        mixed = mixed.astype(BF16).reshape(wide // 2, 2, narrow, block, 2, half)
        return mixed.transpose(0, 4, 2, 1, 3, 5)
    return pl.pallas_call(
        mix_kernel,
        in_specs=[IN_VMEM, IN_VMEM],
        out_specs=IN_HBM,
        out_shape=jax.ShapeDtypeStruct((wide // 2, 2, narrow, 2, block, half), BF16),
        scratch_shapes=[
            pltpu.VMEM((states // LANES, total + 1, size // total + 8, LANES), F32),
            pltpu.VMEM((states // LANES, total + 1, size // total + 8, LANES), F32),
            pltpu.VMEM((2, wide, narrow, block, half), BF16),
            pltpu.SemaphoreType.DMA((2, wide)),
        ],
        compiler_params=kernel_params(16),
        cost_estimate=pl.CostEstimate(flops=2 * size * total * states, bytes_accessed=4 * size * states, transcendentals=0),
        name="mix",
    )(mixing, right_rows)


def apply_kernel(state_ref, own_ref, other_ref, applied_ref):
    outer, cube, high, _, rows, half = state_ref.shape
    pairs = own_ref.shape[0]
    places = itertools.product(range(outer), range(2), range(high))
    state = jnp.concatenate(
        [state_ref[o, :, h, c].reshape(cube * rows, half) for o, c, h in places]
    )
    for side, ref in enumerate((own_ref, other_ref)):
        for q in range(pairs):
            one = jnp.dot(ref[q], state, preferred_element_type=F32).astype(BF16)
            column = (side * pairs + q) * half
            applied_ref[:, column : column + half] = one


def store_term(applied, joined, term_ref):
    outer, cube, high, _, rows, half = term_ref.shape
    joined = joined.reshape(half, -1)
    term = lax.dot_general(applied, joined, (((1,), (1,)), ((), ())), preferred_element_type=F32)
    term = term.astype(term_ref.dtype).reshape(outer, 2, high, cube, rows, half)
    for c in range(2):
        for h in range(high):
            term_ref[:, :, h, c] = term[:, c, h]


def join_kernel(core_ref, applied_ref, comp_ref, keep_ref, send_ref, joined_ref):
    half = keep_ref.shape[-1]
    chips, pairs = comp_ref.shape[0] // 2, comp_ref.shape[1] // 2
    core = core_ref[0]
    for k, (place, term_ref) in enumerate(((1 - core, send_ref), (core, keep_ref))):
        for n in range(2 * pairs):
            pair = n + pairs * (core if n < pairs else -core)
            joined_ref[k, :, :, n * half : (n + 1) * half] = comp_ref[pl.ds(place * chips, chips), pair]
        store_term(applied_ref[...], joined_ref[k], term_ref)


def apply_term_kernel(state_ref, own_ref, other_ref, joined_ref, keep_ref, send_ref, applied_ref):
    apply_kernel(state_ref, own_ref, other_ref, applied_ref)
    for k, term_ref in enumerate((send_ref, keep_ref)):
        store_term(applied_ref[...], joined_ref[k], term_ref)


def last_term_kernel(
    core_ref, state_ref, own_ref, other_ref, joined_ref, keep_ref, send_ref, applied_ref
):
    apply_kernel(state_ref, own_ref, other_ref, applied_ref)
    outer, narrow, _, rows, half = keep_ref.shape
    count = narrow * rows
    core = core_ref[0]
    for c, term_ref in ((1 - core, send_ref), (core, keep_ref)):
        starts = [pl.multiple_of((2 * o + c) * count, count) for o in range(outer)]
        applied = jnp.concatenate([applied_ref[pl.ds(start, count)] for start in starts])
        for k, place in enumerate((1 - core, core)):
            joined = joined_ref[k].reshape(half, -1)
            term = lax.dot_general(applied, joined, (((1,), (1,)), ((), ())), preferred_element_type=F32)
            term = term.astype(term_ref.dtype).reshape(outer, narrow, rows, half)
            term_ref[:, :, place] = term


def local_call(kernel, name, mib, *out, scratch=(), flops=0):
    def call(*operands):
        specs = [
            pl.BlockSpec(memory_space=pltpu.SMEM) if value.dtype == jnp.int32 else IN_VMEM
            for value in operands
        ]
        return pl.pallas_call(
            kernel,
            in_specs=specs,
            out_specs=[IN_VMEM] * len(out),
            out_shape=[jax.ShapeDtypeStruct(*one) for one in out],
            scratch_shapes=scratch,
            compiler_params=kernel_params(mib),
            cost_estimate=pl.CostEstimate(
                flops=flops, bytes_accessed=sum(2 * value.size for value in operands if flops), transcendentals=0
            ),
            name=name,
        )(*operands)

    return call


def apply_pairs(state, own, other):
    pairs, states, _ = own.shape
    half = state.shape[-1]
    if state.shape[-2] % 16:
        full = state.transpose(0, 3, 2, 1, 4, 5).reshape(states, half)
        built = jnp.concatenate([own, other])
        applied = jnp.einsum("sil,lk->isk", built, full, preferred_element_type=F32).astype(BF16)
        return applied.reshape(states, 2 * pairs * half)
    shape = (states, 2 * pairs * half)
    return local_call(apply_kernel, "apply_pairs", 8, (shape, BF16))(state, own, other)[0]


def join_terms(core, applied, comp, shape):
    devices, both, rows, half = comp.shape
    if rows % 16:
        split = comp.reshape(2, devices // 2, 2, both // 2, rows, half)
        split = jnp.stack([split[1 - core], split[core]])
        split = jnp.concatenate([split[:, :, core], split[:, :, 1 - core]], axis=2)
        joined = split.transpose(0, 1, 3, 2, 4).reshape(2, devices // 2, rows, both * half)
        return *terms_of(applied, joined, shape), joined
    out = (shape, F32), (shape, BF16), ((2, devices // 2, rows, both * half), BF16)
    flops = 2 * devices * rows * applied.size
    call = local_call(join_kernel, "join_terms", 12, *out, flops=flops)
    return call(core.reshape(1), applied, comp)


def all_terms(applied, joined, shape):
    outer, cube, high, _, rows, half = shape
    joined = joined.reshape(2, half, -1)
    term = jnp.einsum("ix,kjx->kij", applied, joined, preferred_element_type=F32)
    return term.reshape(2, outer, 2, high, cube, rows, half)


def terms_of(applied, joined, shape):
    term = all_terms(applied, joined, shape).transpose(0, 1, 4, 3, 2, 5, 6)
    return term[1], term[0].astype(BF16)


def apply_and_terms(state, own, other, joined):
    pairs, states, _ = own.shape
    half = state.shape[-1]
    if state.shape[-2] % 16:
        return terms_of(apply_pairs(state, own, other), joined, state.shape)
    scratch = [pltpu.VMEM((states, 2 * pairs * half), BF16)]
    out = (state.shape, F32), (state.shape, BF16)
    flops = 8 * pairs * states**2 * half
    call = local_call(apply_term_kernel, "apply_terms", 12, *out, scratch=scratch, flops=flops)
    return call(state, own, other, joined)


def apply_and_last_terms(core, state, own, other, joined):
    outer, cube, high, _, rows, half = state.shape
    pairs, states, _ = own.shape
    shape = (outer, high * cube, 2, rows, half)
    if rows % 16:
        term = all_terms(apply_pairs(state, own, other), joined, state.shape)
        term = term.reshape(2, outer, 2, high * cube, rows, half)
        term = jnp.where(core == 1, term, term[::-1]).transpose(2, 1, 3, 0, 4, 5)
        return term[core], term[1 - core].astype(BF16)
    scratch = [pltpu.VMEM((states, 2 * pairs * half), BF16)]
    flops = 8 * pairs * states**2 * half
    call = local_call(last_term_kernel, "last_terms", 12, (shape, F32), (shape, BF16), scratch=scratch, flops=flops)
    return call(core.reshape(1), state, own, other, joined)


def local(site_basis, left_ops, right_ops, integrals, wavefunction, pair_order, sector_sizes):
    outer, high, low, near = (lax.axis_size(name) for name in CHIPS)
    narrow = high * low * near
    wide = 2 * outer
    devices = wide * narrow
    rows, states = wavefunction.shape
    half = states // 2
    pairs = left_ops.shape[0]
    pair_total = integrals.shape[0]
    chips = outer * narrow
    own_core, own_high = lax.axis_index(CORE), lax.axis_index(HIGH)
    is_high = own_core == 1

    def own_half(value):
        return jnp.where(is_high, value[..., half:], value[..., :half])

    def other_half(value):
        return jnp.where(is_high, value[..., :half], value[..., half:])

    def by_core(own, other):
        return jnp.stack([jnp.where(is_high, other, own), jnp.where(is_high, own, other)])

    parts = deal_rows(right_ops, devices).reshape(devices, pairs * rows, states)
    parts, wavefunction, site_basis = lax.optimization_barrier((parts, wavefunction, site_basis))
    right_rows = lax.all_to_all(parts, ALL, split_axis=0, concat_axis=0, tiled=True)
    right_rows = right_rows.reshape(pair_total * rows, states)
    mixing = jnp.take(jnp.take(integrals, pair_order, axis=0), pair_order, axis=1)

    blocks = block_ids(sector_sizes, states).astype(F32)
    by_device = blocks.reshape(outer, 2, high, low, near, rows)
    first = (lax.axis_index(OUTER), 0, 0, lax.axis_index(LOW), lax.axis_index(NEAR), 0)
    cube_rows = lax.dynamic_slice(by_device, first, (1, 2, high, 1, 1, rows))
    cube_rows = cube_rows.reshape(2, high, rows).transpose(1, 0, 2)
    own_columns = own_half(blocks)
    cube_mask = (jnp.abs(cube_rows[..., None] - own_columns) <= 2.0).astype(F32)
    local_mask = lax.dynamic_index_in_dim(cube_mask, own_high, 0, keepdims=False)
    own_row = lax.axis_index(ALL) * rows
    own_rows = lax.dynamic_slice_in_dim(blocks, own_row, rows, 0)
    row_mask = (jnp.abs(own_rows[:, None] - blocks.reshape(2, 1, half)) <= 2.0).astype(F32)

    piece = by_core(own_half(wavefunction), swap_cores(other_half(wavefunction)))
    piece = (piece.astype(F32) * local_mask).astype(BF16)
    summed = piece.astype(F32)

    halves = jnp.stack([site_basis[:, :half], site_basis[:, half:]])
    packet = jnp.concatenate([halves, piece])
    packet, cube_mask, row_mask, summed = lax.optimization_barrier(
        (packet, cube_mask, row_mask, summed)
    )
    mixed = mix(mixing, right_rows, wide, narrow, pairs * rows)
    packets, mixed = lax.optimization_barrier((jnp.stack(send_round(packet, (HIGH, LOW), high * low)), mixed))
    slots = []
    for slot in send_round(packets, (OUTER, NEAR), outer * near):
        slots += [slot, swap_cores(slot[:, :2])]
    place = [lax.axis_index((OUTER, NEAR)), lax.axis_index((HIGH, LOW)), own_core]
    basis, state = place_slots(jnp.stack(place), slots, outer, high, near)
    own_built = build(basis.reshape(states, states), left_ops)
    other_built = swap_cores(own_built)
    applied = apply_pairs(state, own_built, other_built)

    mixed = mixed.reshape(devices, 2 * pairs * rows, half)
    comp = lax.all_to_all(mixed, ALL, split_axis=0, concat_axis=0, tiled=True)
    comp = comp.reshape(devices, 2 * pairs, rows, half)

    step_size = 2.0 / math.sqrt(pair_total)
    for order_index in range(1, ORDER):
        if order_index == 1:
            keep, send, joined = join_terms(own_core, applied, comp, state.shape)
        else:
            keep, send = apply_and_terms(state, own_built, other_built, joined)
        partial = (keep + swap_cores(send).astype(F32)).astype(BF16)
        partial = partial.reshape(chips // high, high * 2 * rows, half)
        arrived = lax.all_to_all(partial, CUBE, split_axis=0, concat_axis=0, tiled=True)
        term = jnp.sum(arrived.astype(F32), axis=0).reshape(cube_mask.shape)
        term = add_high(cube_mask * term)
        pieces = (-(step_size / order_index) * cube_mask * term).astype(BF16)
        piece = lax.dynamic_index_in_dim(pieces, own_high, 0, keepdims=False)
        summed = summed + piece.astype(F32)
        copies = jnp.broadcast_to(pieces.reshape(partial.shape[1:]), partial.shape)
        mine = jnp.where(is_high, summed[1], summed[0])
        theirs = jnp.where(is_high, summed[0], summed[1])
        copies, summed, mine, theirs = lax.optimization_barrier((copies, summed, mine, theirs))
        state = lax.all_to_all(copies, CUBE, split_axis=0, concat_axis=0, tiled=True)
        state = state.reshape(outer, low * near, high, 2, rows, half)

    keep, send = apply_and_last_terms(own_core, state, own_built, other_built, joined)
    theirs, send = lax.optimization_barrier((theirs, send))
    theirs, send = lax.optimization_barrier((swap_cores(theirs), swap_cores(send)))
    summed = by_core(mine, theirs)
    partial = (keep + send.astype(F32)).astype(BF16).reshape(chips, 2 * rows, half)
    partial, summed = lax.optimization_barrier((partial, summed))
    arrived = lax.all_to_all(partial, CHIPS, split_axis=0, concat_axis=0, tiled=True)
    term = jnp.sum(arrived.astype(F32), axis=0).reshape(2, rows, half)
    piece = (-(step_size / ORDER) * row_mask * term).astype(BF16)
    summed = summed + piece.astype(F32)
    return jnp.concatenate([summed[0], summed[1]], axis=1)


def solution(mesh):
    wide, narrow = mesh.shape["wide"], mesh.shape["narrow"]
    near = math.gcd(narrow, 2)
    high = math.gcd(narrow // near, 2)
    finer = Mesh(mesh.devices.reshape(wide // 2, 2, high, narrow // near // high, near), ALL)
    placed = (
        P(ALL, None),
        P(ALL, None, None),
        P(ALL, None, None),
        P(),
        P(ALL, None),
        P(),
        P(),
    )
    return jax.shard_map(local, mesh=finer, in_specs=placed, out_specs=P(ALL, None), check_vma=False)
```

```python
import functools
import itertools
import math

import jax
import jax.numpy as jnp
from jax import lax
from jax.experimental import pallas as pl
from jax.experimental.pallas import tpu as pltpu
from jax.sharding import Mesh, PartitionSpec as P

ORDER = 3
OUTER, CORE, HIGH, LOW, NEAR = "outer", "core", "high", "low", "near"
ALL = (OUTER, CORE, HIGH, LOW, NEAR)
CHIPS = (OUTER, HIGH, LOW, NEAR)
CUBE = (OUTER, LOW, NEAR)
MIB = 1024 * 1024
LANES = 128
IN_HBM, IN_VMEM = pl.BlockSpec(memory_space=pltpu.HBM), pl.BlockSpec(memory_space=pltpu.VMEM)
F32, BF16 = jnp.float32, jnp.bfloat16


def whole_block(shape):
    return pl.BlockSpec(shape, lambda *_: (0,) * len(shape))


def kernel_params(mib):
    return pltpu.CompilerParams(vmem_limit_bytes=mib * MIB)


def block_ids(sector_sizes, count):
    ends = jnp.cumsum(sector_sizes)
    ids = jnp.arange(count, dtype=jnp.int32)
    return jnp.sum((ids[:, None] >= ends[None, :]).astype(jnp.int32), axis=1)


def swap_cores(value):
    return lax.ppermute(value, CORE, [(0, 1), (1, 0)])


def add_high(value):
    if lax.axis_size(HIGH) == 1:
        return value
    rounded = value.astype(BF16)
    other = lax.ppermute(rounded, HIGH, [(0, 1), (1, 0)])
    return rounded.astype(F32) + other.astype(F32)


def partner(position, k, size):
    if size & (size - 1):
        return (position + k) % size
    return position ^ k


def send_round(value, axes, size):
    slots = [value]
    for k in range(1, size):
        slots.append(lax.ppermute(value, axes, [(partner(i, k, size), i) for i in range(size)]))
    return slots


def place_kernel(place_ref, *refs):
    slots, (basis_ref, state_ref) = refs[:-2], refs[-2:]
    outer, _, far, near, _, _ = basis_ref.shape
    low = state_ref.shape[1] // near
    half = state_ref.shape[-1]
    across, along, core = place_ref[0], place_ref[1], place_ref[2]
    for j, (own, other) in enumerate(zip(slots[::2], slots[1::2])):
        there = partner(across, j, outer * near)
        o, n = there // near, lax.rem(there, near)
        for k in range(far):
            f = partner(along, k, far)
            for c, slot in ((core, own), (1 - core, other)):
                basis_ref[o, c, f, n, :, :half] = slot[k, 0]
                basis_ref[o, c, f, n, :, half:] = slot[k, 1]
            for c in range(2):
                state_ref[o, lax.rem(f, low) * near + n, f // low, c] = own[k, 2 + c]


def place_slots(place, slots, outer, high, near):
    far, _, rows, half = slots[0].shape
    basis = ((outer, 2, far, near, rows, 2 * half), BF16)
    state = ((outer, far // high * near, high, 2, rows, half), BF16)
    return local_call(place_kernel, "place_slots", 8, basis, state)(place, *slots)


def deal_kernel(right_ref, out_ref, held, in_sems, out_sems):
    pairs, devices = held.shape[:2]
    count = in_sems.shape[1]
    size = devices // count
    places = [(s, g, pl.ds(g * size, size)) for s in range(pairs) for g in range(count)]
    loads = [
        pltpu.make_async_copy(right_ref.at[s, part], held.at[s, part], in_sems.at[s, g])
        for s, g, part in places
    ]
    stores = [
        pltpu.make_async_copy(held.at[s, part], out_ref.at[part, s], out_sems.at[s, g])
        for s, g, part in places
    ]
    for load in loads:
        load.start()
    for load, store in zip(loads, stores):
        load.wait()
        store.start()
    for store in stores:
        store.wait()


def deal_rows(right_ops, devices):
    pairs, states, _ = right_ops.shape
    rows = states // devices
    split = right_ops.reshape(pairs, devices, rows, states)
    if rows % 16:
        return split.transpose(1, 0, 2, 3)
    count = 1
    return pl.pallas_call(
        deal_kernel,
        in_specs=[IN_HBM],
        out_specs=IN_HBM,
        out_shape=jax.ShapeDtypeStruct((devices, pairs, rows, states), BF16),
        scratch_shapes=[
            pltpu.VMEM(split.shape, BF16),
            pltpu.SemaphoreType.DMA((pairs, count)),
            pltpu.SemaphoreType.DMA((pairs, count)),
        ],
        compiler_params=kernel_params(61),
        name="deal_rows",
    )(split)


def build_kernel(basis_ref, own_ref, other_ref, built_ref):
    basis = basis_ref[...]
    pairs = pl.num_programs(0) // 2

    def build_from(left_ref):
        rotated = jnp.dot(left_ref[0], basis, preferred_element_type=F32).astype(BF16)
        built = lax.dot_general(basis, rotated, (((0,), (0,)), ((), ())), preferred_element_type=F32)
        built_ref[0] = built.astype(BF16)

    pl.when(pl.program_id(0) < pairs)(lambda: build_from(own_ref))
    pl.when(pl.program_id(0) >= pairs)(lambda: build_from(other_ref))


def build(basis, own_left, other_left):
    pairs, states, _ = own_left.shape
    return pl.pallas_call(
        build_kernel,
        grid=(2 * pairs,),
        in_specs=[
            whole_block((states, states)),
            pl.BlockSpec((1, states, states), lambda s: (jnp.minimum(s, pairs - 1), 0, 0)),
            pl.BlockSpec((1, states, states), lambda s: (jnp.maximum(s - pairs, 0), 0, 0)),
        ],
        out_specs=pl.BlockSpec((1, states, states), lambda s: (s, 0, 0)),
        out_shape=jax.ShapeDtypeStruct((2 * pairs, states, states), BF16),
        compiler_params=kernel_params(57),
        cost_estimate=pl.CostEstimate(flops=0, bytes_accessed=0, transcendentals=0),
        name="build",
    )(basis, own_left, other_left)


def mix_kernel(mixing_ref, right_ref, out_ref, taken, given, mixed, sems):
    total = mixing_ref.shape[0]
    wide, narrow, block, half = mixed.shape[1:]
    rows = right_ref.shape[0] // total
    lanes = half // LANES
    pitch = taken.shape[2]
    mixing = mixing_ref[...]
    stores = [
        pltpu.make_async_copy(mixed.at[h, w], out_ref.at[w // 2, h, :, w % 2], sems.at[h, w])
        for h in range(2)
        for w in range(wide)
    ]
    for h in range(2):
        places = range(h * lanes, (h + 1) * lanes)
        for place in places:
            part = right_ref[:, place * LANES : (place + 1) * LANES].astype(F32)
            taken[place, :total, :rows] = part.reshape(total, rows, LANES)
        flat_in = [taken.at[place].reshape((total + 1) * pitch, LANES) for place in places]
        flat_out = [given.at[place].reshape((total + 1) * pitch, LANES) for place in places]
        for row in range(rows):
            every = pl.ds(row, total, stride=pitch)
            one = jnp.concatenate([ref[every] for ref in flat_in], axis=1).astype(BF16)
            one = jnp.dot(mixing, one, preferred_element_type=F32)
            for lane, ref in enumerate(flat_out):
                ref[every] = one[:, lane * LANES : (lane + 1) * LANES]
        for lane, place in enumerate(places):
            done = given[place, :total, :rows].astype(BF16).reshape(wide, narrow, block, LANES)
            mixed[h, :, :, :, lane * LANES : (lane + 1) * LANES] = done
        for w in range(wide):
            stores[h * wide + w].start()
    for store in stores:
        store.wait()


def mix(mixing, right_rows, wide, narrow, block):
    size, states = right_rows.shape
    total = mixing.shape[0]
    half = states // 2
    if block % 16:
        mixed = jnp.einsum(
            "st,tx->sx", mixing, right_rows.reshape(total, -1), preferred_element_type=F32
        )
        mixed = mixed.astype(BF16).reshape(wide // 2, 2, narrow, block, 2, half)
        return mixed.transpose(0, 4, 2, 1, 3, 5)
    return pl.pallas_call(
        mix_kernel,
        in_specs=[IN_VMEM, IN_VMEM],
        out_specs=IN_HBM,
        out_shape=jax.ShapeDtypeStruct((wide // 2, 2, narrow, 2, block, half), BF16),
        scratch_shapes=[
            pltpu.VMEM((states // LANES, total + 1, size // total + 8, LANES), F32),
            pltpu.VMEM((states // LANES, total + 1, size // total + 8, LANES), F32),
            pltpu.VMEM((2, wide, narrow, block, half), BF16),
            pltpu.SemaphoreType.DMA((2, wide)),
        ],
        compiler_params=kernel_params(16),
        cost_estimate=pl.CostEstimate(flops=2 * size * total * states, bytes_accessed=4 * size * states, transcendentals=0),
        name="mix",
    )(mixing, right_rows)


def apply_kernel(state_ref, built_ref, applied_ref):
    outer, cube, high, _, rows, half = state_ref.shape
    places = itertools.product(range(outer), range(2), range(high))
    state = jnp.concatenate(
        [state_ref[o, :, h, c].reshape(cube * rows, half) for o, c, h in places]
    )
    for s in range(built_ref.shape[0]):
        one = jnp.dot(built_ref[s], state, preferred_element_type=F32).astype(BF16)
        applied_ref[:, s * half : (s + 1) * half] = one


def store_term(applied, joined, term_ref):
    outer, cube, high, _, rows, half = term_ref.shape
    joined = joined.reshape(half, -1)
    term = lax.dot_general(applied, joined, (((1,), (1,)), ((), ())), preferred_element_type=F32)
    term = term.astype(term_ref.dtype).reshape(outer, 2, high, cube, rows, half)
    for c in range(2):
        for h in range(high):
            term_ref[:, :, h, c] = term[:, c, h]


def join_kernel(core_ref, applied_ref, comp_ref, keep_ref, send_ref, joined_ref):
    half = keep_ref.shape[-1]
    chips, pairs = comp_ref.shape[0] // 2, comp_ref.shape[1] // 2
    core = core_ref[0]
    for k, (place, term_ref) in enumerate(((1 - core, send_ref), (core, keep_ref))):
        for n in range(2 * pairs):
            pair = n + pairs * (core if n < pairs else -core)
            joined_ref[k, :, :, n * half : (n + 1) * half] = comp_ref[pl.ds(place * chips, chips), pair]
        store_term(applied_ref[...], joined_ref[k], term_ref)


def apply_term_kernel(state_ref, built_ref, joined_ref, keep_ref, send_ref, applied_ref):
    apply_kernel(state_ref, built_ref, applied_ref)
    for k, term_ref in enumerate((send_ref, keep_ref)):
        store_term(applied_ref[...], joined_ref[k], term_ref)


def last_term_kernel(
    core_ref, state_ref, built_ref, joined_ref, keep_ref, send_ref, applied_ref
):
    apply_kernel(state_ref, built_ref, applied_ref)
    outer, narrow, _, rows, half = keep_ref.shape
    count = narrow * rows
    core = core_ref[0]
    for c, term_ref in ((1 - core, send_ref), (core, keep_ref)):
        starts = [pl.multiple_of((2 * o + c) * count, count) for o in range(outer)]
        applied = jnp.concatenate([applied_ref[pl.ds(start, count)] for start in starts])
        for k, place in enumerate((1 - core, core)):
            joined = joined_ref[k].reshape(half, -1)
            term = lax.dot_general(applied, joined, (((1,), (1,)), ((), ())), preferred_element_type=F32)
            term = term.astype(term_ref.dtype).reshape(outer, narrow, rows, half)
            term_ref[:, :, place] = term


def local_call(kernel, name, mib, *out, scratch=(), flops=0):
    def call(*operands):
        specs = [
            pl.BlockSpec(memory_space=pltpu.SMEM) if value.dtype == jnp.int32 else IN_VMEM
            for value in operands
        ]
        return pl.pallas_call(
            kernel,
            in_specs=specs,
            out_specs=[IN_VMEM] * len(out),
            out_shape=[jax.ShapeDtypeStruct(*one) for one in out],
            scratch_shapes=scratch,
            compiler_params=kernel_params(mib),
            cost_estimate=pl.CostEstimate(
                flops=flops, bytes_accessed=sum(2 * value.size for value in operands if flops), transcendentals=0
            ),
            name=name,
        )(*operands)

    return call


def apply_pairs(state, built):
    both, states, _ = built.shape
    half = state.shape[-1]
    if state.shape[-2] % 16:
        full = state.transpose(0, 3, 2, 1, 4, 5).reshape(states, half)
        applied = jnp.einsum("sil,lk->isk", built, full, preferred_element_type=F32).astype(BF16)
        return applied.reshape(states, both * half)
    shape = (states, both * half)
    return local_call(apply_kernel, "apply_pairs", 8, (shape, BF16))(state, built)[0]


def join_terms(core, applied, comp, shape):
    devices, both, rows, half = comp.shape
    if rows % 16:
        split = comp.reshape(2, devices // 2, 2, both // 2, rows, half)
        split = jnp.stack([split[1 - core], split[core]])
        split = jnp.concatenate([split[:, :, core], split[:, :, 1 - core]], axis=2)
        joined = split.transpose(0, 1, 3, 2, 4).reshape(2, devices // 2, rows, both * half)
        return *terms_of(applied, joined, shape), joined
    out = (shape, F32), (shape, BF16), ((2, devices // 2, rows, both * half), BF16)
    flops = 2 * devices * rows * applied.size
    call = local_call(join_kernel, "join_terms", 12, *out, flops=flops)
    return call(core.reshape(1), applied, comp)


def all_terms(applied, joined, shape):
    outer, cube, high, _, rows, half = shape
    joined = joined.reshape(2, half, -1)
    term = jnp.einsum("ix,kjx->kij", applied, joined, preferred_element_type=F32)
    return term.reshape(2, outer, 2, high, cube, rows, half)


def terms_of(applied, joined, shape):
    term = all_terms(applied, joined, shape).transpose(0, 1, 4, 3, 2, 5, 6)
    return term[1], term[0].astype(BF16)


def apply_and_terms(state, built, joined):
    both, states, _ = built.shape
    half = state.shape[-1]
    if state.shape[-2] % 16:
        return terms_of(apply_pairs(state, built), joined, state.shape)
    scratch = [pltpu.VMEM((states, both * half), BF16)]
    out = (state.shape, F32), (state.shape, BF16)
    flops = 4 * both * states**2 * half
    call = local_call(apply_term_kernel, "apply_terms", 12, *out, scratch=scratch, flops=flops)
    return call(state, built, joined)


def apply_and_last_terms(core, state, built, joined):
    outer, cube, high, _, rows, half = state.shape
    both, states, _ = built.shape
    shape = (outer, high * cube, 2, rows, half)
    if rows % 16:
        term = all_terms(apply_pairs(state, built), joined, state.shape)
        term = term.reshape(2, outer, 2, high * cube, rows, half)
        term = jnp.where(core == 1, term, term[::-1]).transpose(2, 1, 3, 0, 4, 5)
        return term[core], term[1 - core].astype(BF16)
    scratch = [pltpu.VMEM((states, both * half), BF16)]
    flops = 4 * both * states**2 * half
    call = local_call(last_term_kernel, "last_terms", 12, (shape, F32), (shape, BF16), scratch=scratch, flops=flops)
    return call(core.reshape(1), state, built, joined)


def local(site_basis, left_ops, right_ops, integrals, wavefunction, pair_order, sector_sizes):
    outer, high, low, near = (lax.axis_size(name) for name in CHIPS)
    narrow = high * low * near
    wide = 2 * outer
    devices = wide * narrow
    rows, states = wavefunction.shape
    half = states // 2
    pairs = left_ops.shape[0]
    pair_total = integrals.shape[0]
    chips = outer * narrow
    own_core, own_high = lax.axis_index(CORE), lax.axis_index(HIGH)
    is_high = own_core == 1

    def own_half(value):
        return jnp.where(is_high, value[..., half:], value[..., :half])

    def other_half(value):
        return jnp.where(is_high, value[..., :half], value[..., half:])

    def by_core(own, other):
        return jnp.stack([jnp.where(is_high, other, own), jnp.where(is_high, own, other)])

    parts = deal_rows(right_ops, devices).reshape(devices, pairs * rows, states)
    parts, wavefunction, site_basis = lax.optimization_barrier((parts, wavefunction, site_basis))
    right_rows = lax.all_to_all(parts, ALL, split_axis=0, concat_axis=0, tiled=True)
    right_rows = right_rows.reshape(pair_total * rows, states)
    mixing = jnp.take(jnp.take(integrals, pair_order, axis=0), pair_order, axis=1)

    blocks = block_ids(sector_sizes, states).astype(F32)
    by_device = blocks.reshape(outer, 2, high, low, near, rows)
    first = (lax.axis_index(OUTER), 0, 0, lax.axis_index(LOW), lax.axis_index(NEAR), 0)
    cube_rows = lax.dynamic_slice(by_device, first, (1, 2, high, 1, 1, rows))
    cube_rows = cube_rows.reshape(2, high, rows).transpose(1, 0, 2)
    own_columns = own_half(blocks)
    cube_mask = (jnp.abs(cube_rows[..., None] - own_columns) <= 2.0).astype(F32)
    local_mask = lax.dynamic_index_in_dim(cube_mask, own_high, 0, keepdims=False)
    own_row = lax.axis_index(ALL) * rows
    own_rows = lax.dynamic_slice_in_dim(blocks, own_row, rows, 0)
    row_mask = (jnp.abs(own_rows[:, None] - blocks.reshape(2, 1, half)) <= 2.0).astype(F32)

    piece = by_core(own_half(wavefunction), swap_cores(other_half(wavefunction)))
    piece = (piece.astype(F32) * local_mask).astype(BF16)
    summed = piece.astype(F32)

    halves = jnp.stack([site_basis[:, :half], site_basis[:, half:]])
    packet = jnp.concatenate([halves, piece])
    packet, cube_mask, row_mask, summed = lax.optimization_barrier(
        (packet, cube_mask, row_mask, summed)
    )
    mixed = mix(mixing, right_rows, wide, narrow, pairs * rows)
    packets = jnp.stack(send_round(packet, (HIGH, LOW), high * low))
    packets, mixed, other_left = lax.optimization_barrier((packets, mixed, swap_cores(left_ops)))
    slots = []
    for slot in send_round(packets, (OUTER, NEAR), outer * near):
        slots += [slot, swap_cores(slot[:, :2])]
    place = [lax.axis_index((OUTER, NEAR)), lax.axis_index((HIGH, LOW)), own_core]
    basis, state = place_slots(jnp.stack(place), slots, outer, high, near)
    built = build(basis.reshape(states, states), left_ops, other_left)
    applied = apply_pairs(state, built)

    mixed = mixed.reshape(devices, 2 * pairs * rows, half)
    comp = lax.all_to_all(mixed, ALL, split_axis=0, concat_axis=0, tiled=True)
    comp = comp.reshape(devices, 2 * pairs, rows, half)

    step_size = 2.0 / math.sqrt(pair_total)
    for order_index in range(1, ORDER):
        if order_index == 1:
            keep, send, joined = join_terms(own_core, applied, comp, state.shape)
        else:
            keep, send = apply_and_terms(state, built, joined)
        partial = (keep + swap_cores(send).astype(F32)).astype(BF16)
        partial = partial.reshape(chips // high, high * 2 * rows, half)
        arrived = lax.all_to_all(partial, CUBE, split_axis=0, concat_axis=0, tiled=True)
        term = jnp.sum(arrived.astype(F32), axis=0).reshape(cube_mask.shape)
        term = add_high(cube_mask * term)
        pieces = (-(step_size / order_index) * cube_mask * term).astype(BF16)
        piece = lax.dynamic_index_in_dim(pieces, own_high, 0, keepdims=False)
        summed = summed + piece.astype(F32)
        copies = jnp.broadcast_to(pieces.reshape(partial.shape[1:]), partial.shape)
        mine = jnp.where(is_high, summed[1], summed[0])
        theirs = jnp.where(is_high, summed[0], summed[1])
        copies, summed, mine, theirs = lax.optimization_barrier((copies, summed, mine, theirs))
        state = lax.all_to_all(copies, CUBE, split_axis=0, concat_axis=0, tiled=True)
        state = state.reshape(outer, low * near, high, 2, rows, half)

    keep, send = apply_and_last_terms(own_core, state, built, joined)
    theirs, send = lax.optimization_barrier((theirs, send))
    theirs, send = lax.optimization_barrier((swap_cores(theirs), swap_cores(send)))
    summed = by_core(mine, theirs)
    partial = (keep + send.astype(F32)).astype(BF16).reshape(chips, 2 * rows, half)
    partial, summed = lax.optimization_barrier((partial, summed))
    arrived = lax.all_to_all(partial, CHIPS, split_axis=0, concat_axis=0, tiled=True)
    term = jnp.sum(arrived.astype(F32), axis=0).reshape(2, rows, half)
    piece = (-(step_size / ORDER) * row_mask * term).astype(BF16)
    summed = summed + piece.astype(F32)
    return jnp.concatenate([summed[0], summed[1]], axis=1)


def solution(mesh):
    wide, narrow = mesh.shape["wide"], mesh.shape["narrow"]
    near = math.gcd(narrow, 2)
    high = math.gcd(narrow // near, 2)
    finer = Mesh(mesh.devices.reshape(wide // 2, 2, high, narrow // near // high, near), ALL)
    placed = (
        P(ALL, None),
        P(ALL, None, None),
        P(ALL, None, None),
        P(),
        P(ALL, None),
        P(),
        P(),
    )
    return jax.shard_map(local, mesh=finer, in_specs=placed, out_specs=P(ALL, None), check_vma=False)
```
